256 devices in a mesh: band: 16 (over z, core), comp: 16 (over y, x).
Axes of the slice: x: 4, y: 4, z: 8, core: 2. Of those that a mesh axis runs over, the one named last changes fastest.
Arguments:
- spectrum: float32 [1728, 64, 1440], P('comp', 'band'), may hold values from 0.05 to 2
- group_courant: float32 [48], replicated, may hold values from 0.05 to 0.5
- coupling: bfloat16 [1728, 1728], P('band'), may hold values from -0.15625 to 0.15625
- wind_dir: int32 [64, 1440], P('band'), may hold values from 0 to 35
- sea_mask: int32 [64, 1440], P('band'), may hold values from 0 to 1, as said below
- owner_cells: int32 [256, 270], P(('band', 'comp')), may hold values from 0 to 5759, as said below
- owner_counts: int32 [256], P(('band', 'comp')), may hold values from 135 to 270, as said below
Outputs:
- evolved: float32 [1728, 64, 1440], P('comp', 'band')
The draws below stay inside these ranges and needn't reach their ends.
Inputs may be any that keep to these rules, and one draw needn't show every extreme that they name: `sea_mask`: the land of each band is one run of columns around a centre, widening by row order of a random tie-break; one band has exactly 4320 sea cells, every band at least half of that. `owner_cells`: row b * 16 + c lists the sea cells owned by owner c of band b as row within the band * 1440 + longitude. The first owner_counts entries are the owner's cells in increasing order, the owners of a band take consecutive runs of the band's sea cells in order, every sea cell is listed exactly once, and the remaining entries are 0. `owner_counts`: the counts of the owners of one band differ by at most one and sum to the band's sea cells.
All inputs are finite; a program needn't handle non-finite values.
Results may differ from the reference program's by a relative error of at most 0.0014.
Values may be sent and summed in bfloat16 or wider, within the bound.
A program may use at most 192 MiB of HBM per device.

```python
import math
import jax
import jax.numpy as jnp
from jax import lax

DIRS = 36
FREQS = 48
LON = 1440
ROWS = 4
SUBSTEPS = 3
COMPS = 1728
LAT = 64
CAP = 270
OWNERS = 256
N_BAND = 16
N_COMP = 16


def sea_layout(key):
    bands = LAT // ROWS
    comp_devs = OWNERS // bands
    cells = ROWS * LON
    full_sea = comp_devs * CAP
    key_full, key_drop, key_center, key_order = jax.random.split(key, 4)
    full_band = jax.random.randint(key_full, (), 0, bands)
    drops = jax.random.randint(key_drop, (bands,), 0, full_sea // 2 + 1)
    sea_count = full_sea - jnp.where(jnp.arange(bands) == full_band, 0, drops)
    centers = jax.random.randint(key_center, (bands,), 0, LON)
    column = jnp.arange(cells, dtype=jnp.int32) % LON
    spread = jnp.abs(column[None, :] - centers[:, None])
    distance = jnp.minimum(spread, LON - spread)
    order_keys = jax.random.split(key_order, bands)
    shuffle = jax.vmap(lambda part_key: jax.random.permutation(part_key, cells))(order_keys)
    score = distance * cells + shuffle.astype(jnp.int32)
    ranking = jnp.argsort(jnp.argsort(score, axis=1), axis=1)
    land_count = cells - sea_count
    sea = (ranking >= land_count[:, None]).astype(jnp.int32)
    return (sea, sea_count)


def owner_layout(key):
    bands = LAT // ROWS
    comp_devs = OWNERS // bands
    cells = ROWS * LON
    sea, sea_count = sea_layout(key)
    cell_index = jnp.arange(cells, dtype=jnp.int32)
    sea_order = jnp.argsort(jnp.where(sea == 1, cell_index[None, :], cell_index[None, :] + cells), axis=1).astype(jnp.int32)
    base = sea_count // comp_devs
    extra = sea_count % comp_devs
    owner = jnp.arange(comp_devs, dtype=jnp.int32)
    counts = base[:, None] + (owner[None, :] < extra[:, None]).astype(jnp.int32)
    starts = owner[None, :] * base[:, None] + jnp.minimum(owner[None, :], extra[:, None])
    slot = jnp.arange(CAP, dtype=jnp.int32)
    position = jnp.minimum(starts[:, :, None] + slot[None, None, :], cells - 1)
    listed = jax.vmap(lambda order, place: jnp.take(order, place))(sea_order, position)
    listed = jnp.where(slot[None, None, :] < counts[:, :, None], listed, 0)
    return (listed.reshape(OWNERS, CAP).astype(jnp.int32), counts.reshape(OWNERS).astype(jnp.int32))


def draw_sea_mask(key, part):
    sea, sea_count = sea_layout(key)
    return sea.reshape(LAT, LON)


def draw_owner_cells(key, part):
    listed, counts = owner_layout(key)
    return listed


def draw_owner_counts(key, part):
    listed, counts = owner_layout(key)
    return counts


def set_ends(array, rng, low, high):
    spot = [jax.random.randint(jax.random.fold_in(rng, axis), (), 0, length) for axis, length in enumerate(array.shape)]
    longest = array.shape.index(max(array.shape))
    next_to = spot[:longest] + [(spot[longest] + 1) % array.shape[longest]] + spot[longest + 1:]
    return array.at[tuple(spot)].set(low).at[tuple(next_to)].set(high)


def shard_levels(key, shape, cuts, least, largest):
    gain = 1.0
    for axis_at, blocks in cuts:
        heights = jax.random.uniform(jax.random.fold_in(jax.random.fold_in(key, 6), axis_at), (blocks,), jnp.float32, least / len(cuts), largest / len(cuts))
        gain = gain * jnp.repeat(jnp.exp(heights), shape[axis_at] // blocks).reshape((-1,) + (1,) * (len(shape) - 1 - axis_at))
    return gain


def scatter_about(key, shape, width, reach, cuts=(), kind=jnp.bfloat16):
    array = width * jax.random.normal(key, shape, jnp.float32)
    if cuts:
        array = array * shard_levels(key, shape, cuts, -0.22, 0.18)
    return jnp.clip(array, -reach, reach).astype(kind)


def setup_inputs(seed: int = 0) -> dict:
    seeds = jax.random.split(jax.random.key(seed), 8)
    return {
        "spectrum": jnp.clip(jnp.exp(math.log(2.0) - 3.6888794 * jax.random.uniform(seeds[0], (COMPS, LAT, LON), jnp.float32) ** shard_levels(seeds[0], (COMPS, LAT, LON), ((0, 16), (1, 16)), -0.2, 0.2)), 0.05, 2.0),
        "group_courant": jnp.clip(jnp.exp(jax.random.uniform(seeds[1], (FREQS,), jnp.float32, math.log(0.05), math.log(0.5))), 0.05, 0.5),
        "coupling": scatter_about(seeds[2], (COMPS, COMPS), COMPS ** -0.5, 0.15625, ((0, 16),)),
        "wind_dir": set_ends(jax.random.randint(seeds[3], (LAT, LON), 0, DIRS), jax.random.fold_in(seeds[3], 1), 0, DIRS - 1).astype(jnp.int32),
        "sea_mask": draw_sea_mask(jax.random.fold_in(seeds[7], 71), 0),
        "owner_cells": draw_owner_cells(jax.random.fold_in(seeds[7], 71), 0),
        "owner_counts": draw_owner_counts(jax.random.fold_in(seeds[7], 71), 0),
    }


first_lat = 30.0
step_time = 0.5
wind_gain = 0.6
damping = 0.4


def courant_rows(group_courant, comp_index, row_index):
    freq = comp_index % FREQS
    dirn = comp_index // FREQS
    picker = (freq[:, None] == jnp.arange(FREQS, dtype=jnp.int32)[None, :]).astype(jnp.float32)
    speed = jnp.sum(picker * group_courant[None, :], axis=1)
    theta = (2.0 * math.pi / DIRS) * dirn.astype(jnp.float32)
    latitude = (first_lat + 0.25 * (row_index.astype(jnp.float32) + 0.5)) * (math.pi / 180.0)
    cross_x = (speed * jnp.cos(theta))[:, None, None] / jnp.cos(latitude)[None, :, None]
    cross_y = (speed * jnp.sin(theta))[:, None, None]
    return cross_x, cross_y


def advect(field, south, north, sea, cross_x, cross_y):
    west = jnp.roll(field, 1, axis=2)
    east = jnp.roll(field, -1, axis=2)
    moved = field - jnp.maximum(cross_x, 0.0) * (field - west) - jnp.minimum(cross_x, 0.0) * (east - field)
    moved = moved - jnp.maximum(cross_y, 0.0) * (field - south) - jnp.minimum(cross_y, 0.0) * (north - field)
    return moved * sea


def sources(owned, wind_index, transfer):
    comps = owned.shape[0]
    dirn = jnp.arange(comps, dtype=jnp.int32) // FREQS
    angle = (2.0 * math.pi / DIRS) * (dirn[:, None] - wind_index[None, :]).astype(jnp.float32)
    facing = jnp.maximum(jnp.cos(angle), 0.0)
    energy = jnp.sum(owned, axis=0) / comps
    growth = wind_gain * facing * owned - damping * energy[None, :] * owned + transfer
    return jnp.maximum(owned + step_time * growth, 0.0)


def reference(spectrum, group_courant, coupling, wind_dir, sea_mask, owner_cells, owner_counts):
    comps = DIRS * FREQS
    cells = ROWS * LON
    cross_x, cross_y = courant_rows(group_courant, jnp.arange(comps, dtype=jnp.int32), jnp.arange(LAT, dtype=jnp.int32))
    sea = sea_mask.astype(jnp.float32)[None]
    field = spectrum
    for step in range(SUBSTEPS):
        south = jnp.pad(field[:, :-1], ((0, 0), (1, 0), (0, 0)))
        north = jnp.pad(field[:, 1:], ((0, 0), (0, 1), (0, 0)))
        field = advect(field, south, north, sea, cross_x, cross_y)
    banded = jnp.moveaxis(field.reshape(comps, N_BAND, cells), 1, 0)
    winds = wind_dir.reshape(N_BAND, cells)
    lists = owner_cells.reshape(N_BAND, N_COMP * CAP)
    counts = owner_counts.reshape(N_BAND, N_COMP)
    alive_all = (jnp.arange(CAP, dtype=jnp.int32)[None, None, :] < counts[:, :, None]).reshape(N_BAND, N_COMP * CAP)

    def one_band(inputs):
        block, wind, listed, alive = inputs
        owned = jnp.take(block, listed, axis=1)
        squared = (owned * owned).astype(jnp.bfloat16)
        transfer = jnp.dot(coupling, squared, preferred_element_type=jnp.float32)
        updated = sources(owned, jnp.take(wind, listed), transfer)
        target = jnp.where(alive, listed, cells)
        return jnp.zeros((comps, cells), jnp.float32).at[:, target].set(updated, mode="drop")

    evolved = lax.map(one_band, (banded, winds, lists, alive_all))
    return jnp.moveaxis(evolved, 0, 1).reshape(comps, LAT, LON)
```

```python
import math

import jax
import jax.numpy as jnp
from jax import lax
from jax.experimental import pallas as pl
from jax.experimental.pallas import tpu as pltpu
from jax.sharding import PartitionSpec as P

DIRS = 36
FREQS = 48
COMPS = 1728
LON = 1440
ROWS = 4
NB = 16
KD = COMPS // NB
KP = 112
LP = 1536
KALL = NB * KP
QW = LP // 4
HALF = KALL // 2
CH = 16
NCH = KP // CH

first_lat = 30.0
step_time = 0.5
wind_gain = 0.6
damping = 0.4

MESH = pl.DeviceIdType.MESH
F32 = jnp.float32
BF16 = jnp.bfloat16


def lane_iota(shape):
    return lax.broadcasted_iota(jnp.int32, shape, 1)


def row_iota(shape):
    return lax.broadcasted_iota(jnp.int32, shape, 0)


def kernel(
    spec, coup, coef, aux, out,
    raw, f, hs, hr, mh, stage, S, C, tst, trv, eacc,
    load_sem, hs_sem, hr_sem, ms_sem, mr_sem, ss_sem, sr_sem, ts_sem, tr_sem,
    cs_sem, ring_sem, xy_sem, sib_sem,
):
    b = lax.axis_index("band")
    c = lax.axis_index("comp")
    core = b % 2
    y, x = c // 4, c % 4
    up = c < 8
    dirn = jnp.where(up, 1, -1)
    west = jnp.logical_or(c < 4, c >= 12)
    has_send = jnp.where(up, b < 15, b > 0)
    has_recv = jnp.where(up, b > 0, b < 15)
    to_band = (b + dirn + 16) % 16
    sib = b + 1 - 2 * core
    half = (x + y) % 2

    def row_of(i):
        return jnp.where(up, i, 3 - i)

    def load(i):
        return pltpu.make_async_copy(spec.at[:, row_of(i), :], raw.at[i], load_sem.at[i])

    for i in range(ROWS):
        load(i).start()

    barrier = pltpu.get_barrier_semaphore()

    @pl.loop(1, NB)
    def _(n):
        pl.semaphore_signal(barrier, inc=1, device_id={"comp": (c + n) % 16}, device_id_type=MESH)

    for n in (1, 2, 14, 15):
        pl.semaphore_signal(barrier, inc=1, device_id={"band": (b + n) % 16}, device_id_type=MESH)

    def pad_cols(v):
        n = v.shape[0]
        parts = []
        for s in range(NB):
            parts.append(v[:, s * KD : (s + 1) * KD])
            parts.append(jnp.zeros((n, KP - KD), F32))
        return jnp.concatenate(parts, axis=1)

    @pl.loop(0, NCH - 1)
    def _(g):
        rows = pl.ds(pl.multiple_of(g * CH, CH), CH)
        C[b, rows, :] = pad_cols(coup[rows, :].astype(F32)).astype(BF16)

    tail = pad_cols(coup[KD - 12 :, :].astype(F32))
    tail = jnp.concatenate([tail, jnp.zeros((4, KALL), F32)], axis=0)
    spot = lane_iota((CH, KALL)) % KP
    ones = jnp.logical_and(spot >= KD, spot < KD + 3)
    ones = jnp.logical_and(ones, row_iota((CH, KALL)) == 12)
    C[b, pl.ds(KP - CH, CH), :] = jnp.where(ones, 1.0, tail).astype(BF16)

    for i in range(ROWS):
        load(i).wait()

    pl.semaphore_wait(barrier, NB - 1 + 4)

    mask_copy = pltpu.make_async_remote_copy(
        src_ref=aux.at[pl.ds(2, 2)], dst_ref=mh, send_sem=ms_sem, recv_sem=mr_sem,
        device_id={"band": to_band}, device_id_type=MESH,
    )

    def halo(j):
        rows = pl.ds(pl.multiple_of(j * CH, CH), CH)
        return pltpu.make_async_remote_copy(
            src_ref=hs.at[:, rows, :], dst_ref=hr.at[:, rows, :],
            send_sem=hs_sem, recv_sem=hr_sem.at[j],
            device_id={"band": to_band}, device_id_type=MESH,
        )

    @pl.when(has_send)
    def _():
        mask_copy.start()

    def build(j, count):
        rows = pl.ds(pl.multiple_of(j * CH, CH), CH)
        for i in range(ROWS):
            v = raw[i, pl.ds(pl.multiple_of(j * CH, CH), count), :]
            v = jnp.concatenate([v, v[:, :48], v[:, LON - 48 :]], axis=1)
            if count < CH:
                v = jnp.concatenate([v, jnp.zeros((CH - count, LP), F32)], axis=0)
            f[3 + i, rows, :] = v
            if i > 0:
                hs[i - 1, rows, :] = v.astype(BF16)

        @pl.when(has_send)
        def _():
            halo(j).start()

    @pl.loop(0, NCH - 1)
    def _(j):
        build(j, CH)

    build(NCH - 1, KD - CH * (NCH - 1))

    mine = pl.ds(pl.multiple_of(half * HALF, 128), HALF)
    theirs = pl.ds(pl.multiple_of((1 - half) * HALF, 128), HALF)

    def ring(block, step, n):
        return pltpu.make_async_remote_copy(
            src_ref=C.at[block, :, mine], dst_ref=C.at[block, :, mine],
            send_sem=cs_sem, recv_sem=ring_sem.at[n],
            device_id={"band": (b + step + 32) % 16}, device_id_type=MESH,
        )

    xy = (
        y * 4 + (x + 1) % 4,
        y * 4 + (x + 3) % 4,
        ((y + 1) % 4) * 4 + x,
        ((y + 3) % 4) * 4 + x,
    )

    def spread(block, at):
        for k, (lo, cnt) in enumerate(((0, 32), (32, 32), (64, 32), (96, 16))):
            piece = C.at[block, pl.ds(lo, cnt), mine]
            pltpu.make_async_remote_copy(
                src_ref=piece, dst_ref=piece, send_sem=cs_sem, recv_sem=xy_sem.at[at],
                device_id={"comp": xy[k]}, device_id_type=MESH,
            ).start()

    def to_sib(block, cols, n):
        return pltpu.make_async_remote_copy(
            src_ref=C.at[block, :, cols], dst_ref=C.at[block, :, cols],
            send_sem=cs_sem, recv_sem=sib_sem.at[n],
            device_id={"band": sib}, device_id_type=MESH,
        )

    events = ((1, 1), (-1, 1), (1, 2), (-1, 2), (1, 3), (1, 4), (1, 5))
    last = {1: 5, -1: 2}

    def block_of(side, s, base=None):
        base = b if base is None else base
        return (base + 2 * side * s * dirn + 32) % 16

    def distance(side, s):
        return (side * s * dirn + 8) % 8 - 1

    def ring_event(n):
        side, s = events[n]
        block = block_of(side, s)
        ring(block, 0, n).wait_recv()
        if s < last[side]:
            ring(block, -2 * side * dirn, events.index((side, s + 1))).start()
        spread(block, distance(side, s))
        to_sib(block, mine, n).start()

    def xy_event(n):
        side, s = events[n]
        block = block_of(side, s)
        whole = C.at[block, :, theirs]
        pltpu.make_async_copy(whole, whole, xy_sem.at[distance(side, s)]).wait()
        to_sib(block, theirs, n).start()

    ring(b, -2 * dirn, 0).start()
    ring(b, 2 * dirn, 1).start()
    to_sib(b, pl.ds(0, KALL), 7).start()

    def advect(rows, shift):
        cols = [coef[rows, p : p + 1] for p in range(8)]
        for s in range(3):
            for p in range(6, s, -1):
                v = f[p, rows, :]
                moved = v - cols[p] * (v - pltpu.roll(v, shift, 1)) - cols[7] * (v - f[p - 1, rows, :])
                f[p, rows, :] = moved * (mh[p - 1] if p < 3 else aux[p - 3])

    eacc[...] = jnp.zeros_like(eacc)

    @pl.when(has_recv)
    def _():
        mask_copy.wait_recv()

    @pl.when(jnp.logical_not(has_recv))
    def _():
        mh[...] = jnp.zeros_like(mh)

    def send_squares(j):
        rows = pl.ds(pl.multiple_of(j * CH, CH), CH)
        place = pl.ds(pl.multiple_of(c * KP + j * CH, CH), CH)

        @pl.loop(1, NB)
        def _(n):
            to = (c + n) % 16
            pltpu.make_async_remote_copy(
                src_ref=stage.at[to, rows, :], dst_ref=S.at[place, :],
                send_sem=ss_sem, recv_sem=sr_sem,
                device_id={"comp": to}, device_id_type=MESH,
            ).start()

    def chunk(j, final):
        rows = pl.ds(pl.multiple_of(j * CH, CH), CH)

        @pl.when(has_recv)
        def _():
            halo(j).wait_recv()
            for p in range(3):
                f[p, rows, :] = hr[p, rows, :].astype(F32)

        @pl.when(jnp.logical_not(has_recv))
        def _():
            for p in range(3):
                f[p, rows, :] = jnp.zeros((CH, LP), F32)

        @pl.when(west)
        def _():
            for h in range(2):
                advect(pl.ds(pl.multiple_of(j * CH + 8 * h, 8), 8), 1)

        @pl.when(jnp.logical_not(west))
        def _():
            for h in range(2):
                advect(pl.ds(pl.multiple_of(j * CH + 8 * h, 8), 8), LP - 1)

        for i in range(ROWS):
            for q in range(4):
                lanes = pl.ds(q * QW, QW)
                v = f[3 + i, rows, lanes]
                sq = v * v
                e = eacc[i, :, lanes] + v[:8] + v[8:]
                if final:
                    total = jnp.sum(e, axis=0, keepdims=True)
                    hi = total.astype(BF16).astype(F32)
                    mid = (total - hi).astype(BF16).astype(F32)
                    lo = total - hi - mid
                    at = row_iota((CH, QW))
                    sq = jnp.where(at == 12, hi, jnp.where(at == 13, mid, jnp.where(at == 14, lo, sq)))
                else:
                    eacc[i, :, lanes] = e
                stage[4 * row_of(i) + q, rows, :] = sq.astype(BF16)
        send_squares(j)

    for j in range(NCH - 1):
        chunk(j, False)
        ring_event(j)
        if 0 < j < 5:
            xy_event(j - 1)
    chunk(NCH - 1, True)
    ring_event(NCH - 1)
    for n in range(4, NCH):
        xy_event(n)

    S[pl.ds(pl.multiple_of(c * KP, CH), KP), :] = stage[c]
    for n in range(NCH):
        side, s = events[n]
        block = block_of(side, s, sib)
        to_sib(block, pl.ds(0, KALL), n).wait_recv()
    to_sib(sib, pl.ds(0, KALL), 7).wait_recv()
    rest = S.at[pl.ds(0, (NB - 1) * KP), :]
    pltpu.make_async_copy(rest, rest, sr_sem).wait()

    def back(to):
        return pltpu.make_async_remote_copy(
            src_ref=tst.at[to], dst_ref=trv.at[c], send_sem=ts_sem, recv_sem=tr_sem.at[c],
            device_id={"comp": to}, device_id_type=MESH,
        )

    def code(t):
        at = row_iota((KP, QW))
        mean = t[KD : KD + 1] * (1.0 / COMPS)
        t = jnp.maximum(t, -6.0)
        top = jnp.max(jnp.where(at < KD, jnp.abs(t), 0.0), axis=0, keepdims=True)
        power = jnp.ceil(jnp.log2(jnp.maximum(top, 1e-12)) + 0.01)
        scaled = t * (32000.0 * jnp.exp2(-power))
        hi = jnp.floor(mean * 16000.0)
        lo = (mean * 16000.0 - hi) * 32000.0
        scaled = jnp.where(at < KD, scaled, jnp.where(at == KD, power, jnp.where(at == KD + 1, hi, lo)))
        return jnp.round(scaled).astype(jnp.int32).astype(jnp.int16)

    @pl.loop(0, NB // 2)
    def _(n):
        pair = (c // 2 + n) % 8
        lhs = C[pl.ds(pair * 2, 2)].reshape(2 * KP, KALL)
        t = jnp.dot(lhs, S[...], preferred_element_type=F32)
        for k in range(2):
            to = pair * 2 + k
            tst[to] = code(t[k * KP : (k + 1) * KP])

            @pl.when(to != c)
            def _():
                back(to).start()

    trv[c] = tst[c]

    for i in range(ROWS):
        r = row_of(i)
        for q in range(4):
            o = 4 * r + q
            lanes = pl.ds(q * QW, QW)

            @pl.when(o != c)
            def _():
                pltpu.make_async_copy(tst.at[o], trv.at[o], tr_sem.at[o]).wait()

            info = trv[o, pl.ds(KP - CH, CH), :].astype(jnp.int32).astype(F32)
            scale = jnp.exp2(info[12:13]) * (step_time / 32000.0)
            energy = (info[13:14] + info[14:15] * (1.0 / 32000.0)) * (step_time * damping / 16000.0)
            mask = aux[i, :, lanes]
            cosw = aux[4 + i, :, lanes]
            sinw = aux[8 + i, :, lanes]
            width = min(QW, LON - q * QW)

            def update(j, count):
                rows = pl.ds(pl.multiple_of(j * CH, CH), CH)
                t = trv[o, rows, :].astype(jnp.int32).astype(F32)
                v = f[3 + i, rows, lanes]
                facing = jnp.maximum(coef[rows, 8:9] * cosw + coef[rows, 9:10] * sinw, 0.0)
                new = v + ((step_time * wind_gain) * facing - energy) * v + t * scale
                new = jnp.maximum(new, 0.0) * mask
                out[r, pl.ds(pl.multiple_of(j * CH, CH), count), pl.ds(q * QW, width)] = new[:count, :width]

            @pl.loop(0, NCH - 1)
            def _(j):
                update(j, CH)

            update(NCH - 1, KD - CH * (NCH - 1))

    @pl.when(has_send)
    def _():
        mask_copy.wait_send()
        pltpu.make_async_copy(hs, hs, hs_sem).wait()

    sent = C.at[pl.ds(0, 15)]
    pltpu.make_async_copy(sent, sent, cs_sem).wait()
    pltpu.make_async_copy(rest, rest, ss_sem).wait()
    tsent = tst.at[pl.ds(0, 15)]
    pltpu.make_async_copy(tsent, tsent, ts_sem).wait()


def body(spectrum, group_courant, coupling, wind_dir, sea_mask, owner_cells, owner_counts):
    b = lax.axis_index("band")
    c = lax.axis_index("comp")
    up = c < 8
    local = jnp.arange(KP, dtype=jnp.int32)
    index = c * KD + local
    freq = index % FREQS
    dirn = index // FREQS
    picker = (freq[:, None] == jnp.arange(FREQS, dtype=jnp.int32)[None, :]).astype(F32)
    speed = jnp.sum(picker * group_courant[None, :], axis=1)
    speed = jnp.where(local < KD, speed, 0.0)
    theta = 2.0 * math.pi / DIRS * dirn.astype(F32)
    plane = jnp.arange(7, dtype=jnp.int32)
    row = b * ROWS + jnp.where(up, plane - 3, 6 - plane)
    latitude = (first_lat + 0.25 * (row.astype(F32) + 0.5)) * (math.pi / 180.0)
    cosd, sind = jnp.cos(theta)[:, None], jnp.sin(theta)[:, None]
    cross_x = jnp.abs(speed[:, None] * cosd) / jnp.cos(latitude)[None, :]
    cross_y = jnp.abs(speed[:, None] * sind)
    coef = jnp.concatenate([cross_x, cross_y, cosd, sind, jnp.zeros((KP, 6), F32)], axis=1)
    angle = 2.0 * math.pi / DIRS * wind_dir.astype(F32)
    aux = jnp.concatenate([
        jnp.where(up, v, v[::-1]) for v in (sea_mask.astype(F32), jnp.cos(angle), jnp.sin(angle))
    ], axis=0)
    aux = jnp.concatenate([aux, aux[:, :48], aux[:, LON - 48 :]], axis=1).reshape(12, 1, LP)

    vmem = pl.BlockSpec(memory_space=pltpu.VMEM)
    dma = pltpu.SemaphoreType.DMA
    out = pl.pallas_call(
        kernel,
        out_shape=jax.ShapeDtypeStruct((ROWS, KD, LON), F32),
        in_specs=[pl.BlockSpec(memory_space=pl.ANY), vmem, vmem, vmem],
        out_specs=vmem,
        scratch_shapes=[
            pltpu.VMEM((ROWS, KD, LON), F32),
            pltpu.VMEM((7, KP, LP), F32),
            pltpu.VMEM((3, KP, LP), BF16),
            pltpu.VMEM((3, KP, LP), BF16),
            pltpu.VMEM((2, 1, LP), F32),
            pltpu.VMEM((NB, KP, QW), BF16),
            pltpu.VMEM((KALL, QW), BF16),
            pltpu.VMEM((NB, KP, KALL), BF16),
            pltpu.VMEM((NB, KP, QW), jnp.int16),
            pltpu.VMEM((NB, KP, QW), jnp.int16),
            pltpu.VMEM((ROWS, 8, LP), F32),
            dma((ROWS,)), dma, dma((NCH,)), dma, dma, dma, dma, dma, dma((NB,)),
            dma, dma((7,)), dma((7,)), dma((8,)),
        ],
        compiler_params=pltpu.CompilerParams(
            collective_id=0, has_side_effects=True, vmem_limit_bytes=56 * 2**20
        ),
        cost_estimate=pl.CostEstimate(
            flops=2 * KALL * KALL * QW, bytes_accessed=12 * 2**20, transcendentals=0
        ),
    )(spectrum, coupling, coef, aux)
    return jnp.transpose(out, (1, 0, 2))


def solution(mesh):
    return jax.shard_map(
        body,
        mesh=mesh,
        in_specs=(
            P("comp", "band", None),
            P(),
            P("band", None),
            P("band", None),
            P("band", None),
            P(("band", "comp"), None),
            P(("band", "comp")),
        ),
        out_specs=P("comp", "band", None),
        check_vma=False,
    )
```

```python
import math

import jax
import jax.numpy as jnp
from jax import lax
from jax.experimental import pallas as pl
from jax.experimental.pallas import tpu as pltpu
from jax.sharding import PartitionSpec as P

DIRS = 36
FREQS = 48
COMPS = 1728
LON = 1440
ROWS = 4
NB = 16
KD = COMPS // NB
KP = 112
LP = 1536
KALL = NB * KP
QW = LP // 4
HALF = KALL // 2
CH = 16
NCH = KP // CH

first_lat = 30.0
step_time = 0.5
wind_gain = 0.6
damping = 0.4

MESH = pl.DeviceIdType.MESH
F32 = jnp.float32
BF16 = jnp.bfloat16


def lane_iota(shape):
    return lax.broadcasted_iota(jnp.int32, shape, 1)


def row_iota(shape):
    return lax.broadcasted_iota(jnp.int32, shape, 0)


def kernel(
    spec, gc, coup, wind, sea, out,
    raw, f, hs, hr, coef, aux, mrow, mh, mask_h, stage, S, C, tst, trv, eacc,
    load_sem, hs_sem, hr_sem, ms_sem, mr_sem, ss_sem, sr_sem, ts_sem, tr_sem,
    cs_sem, ring_sem, xy_sem, sib_sem, out_sem,
):
    b = lax.axis_index("band")
    c = lax.axis_index("comp")
    z, core = b // 2, b % 2
    y, x = c // 4, c % 4
    up = c < 8
    dirn = jnp.where(up, 1, -1)
    west = jnp.logical_or(c < 4, c >= 12)
    has_send = jnp.where(up, b < 15, b > 0)
    has_recv = jnp.where(up, b > 0, b < 15)
    to_band = (b + dirn + 16) % 16
    sib = b + 1 - 2 * core
    half = (x + y) % 2

    def row_of(i):
        return jnp.where(up, i, 3 - i)

    def rows_at(j, count=CH):
        return pl.ds(pl.multiple_of(j * CH, CH), count)

    def load(j, i):
        count = CH if j < NCH - 1 else KD - CH * (NCH - 1)
        return pltpu.make_async_copy(
            spec.at[pl.ds(j * CH, count), row_of(i), :],
            raw.at[i, pl.ds(j * CH, count), :],
            load_sem.at[j, i],
        )

    for j in range(NCH):
        for i in range(ROWS):
            load(j, i).start()

    barrier = pltpu.get_barrier_semaphore()

    @pl.loop(1, NB)
    def _(n):
        pl.semaphore_signal(barrier, inc=1, device_id={"comp": (c + n) % 16}, device_id_type=MESH)

    for n in (1, 2, 14, 15):
        pl.semaphore_signal(barrier, inc=1, device_id={"band": (b + n) % 16}, device_id_type=MESH)

    def pad_cols(v):
        n = v.shape[0]
        parts = []
        for s in range(NB):
            parts.append(v[:, s * KD : (s + 1) * KD])
            parts.append(jnp.zeros((n, KP - KD), F32))
        return jnp.concatenate(parts, axis=1)

    @pl.loop(0, NCH - 1)
    def _(g):
        C[b, rows_at(g), :] = pad_cols(coup[rows_at(g), :].astype(F32)).astype(BF16)

    tail = pad_cols(coup[KD - 12 :, :].astype(F32))
    tail = jnp.concatenate([tail, jnp.zeros((4, KALL), F32)], axis=0)
    spot = lane_iota((CH, KALL)) % KP
    ones = jnp.logical_and(spot >= KD, spot < KD + 3)
    ones = jnp.logical_and(ones, row_iota((CH, KALL)) == 12)
    C[b, pl.ds(KP - CH, CH), :] = jnp.where(ones, 1.0, tail).astype(BF16)

    def wrap(v):
        return jnp.concatenate([v, v[:, :48], v[:, LON - 48 :]], axis=1)

    seas = wrap(sea[...].astype(F32))
    angle = 2.0 * math.pi / DIRS * wind[...].astype(F32)
    cosw, sinw = wrap(jnp.cos(angle)), wrap(jnp.sin(angle))
    for r in range(ROWS):
        for k, v in enumerate((seas, cosw, sinw)):
            aux[4 * k + row_of(r)] = jnp.broadcast_to(v[r : r + 1], (8, LP))
        mrow[row_of(r)] = seas[r : r + 1]

    pl.semaphore_wait(barrier, NB - 1 + 4)

    mask_copy = pltpu.make_async_remote_copy(
        src_ref=mrow.at[pl.ds(2, 2)], dst_ref=mh, send_sem=ms_sem, recv_sem=mr_sem,
        device_id={"band": to_band}, device_id_type=MESH,
    )

    def halo(j):
        rows = rows_at(j)
        return pltpu.make_async_remote_copy(
            src_ref=hs.at[:, rows, :], dst_ref=hr.at[:, rows, :],
            send_sem=hs_sem, recv_sem=hr_sem.at[j],
            device_id={"band": to_band}, device_id_type=MESH,
        )

    mine = pl.ds(pl.multiple_of(half * HALF, 128), HALF)
    theirs = pl.ds(pl.multiple_of((1 - half) * HALF, 128), HALF)

    def ring(block, step, n):
        return pltpu.make_async_remote_copy(
            src_ref=C.at[block, :, mine], dst_ref=C.at[block, :, mine],
            send_sem=cs_sem, recv_sem=ring_sem.at[n],
            device_id={"band": (b + step + 32) % 16}, device_id_type=MESH,
        )

    xy = (
        y * 4 + (x + 1) % 4,
        y * 4 + (x + 3) % 4,
        ((y + 1) % 4) * 4 + x,
        ((y + 3) % 4) * 4 + x,
    )

    def spread(block, at):
        for k, (lo, cnt) in enumerate(((0, 32), (32, 32), (64, 32), (96, 16))):
            piece = C.at[block, pl.ds(lo, cnt), mine]
            pltpu.make_async_remote_copy(
                src_ref=piece, dst_ref=piece, send_sem=cs_sem, recv_sem=xy_sem.at[at],
                device_id={"comp": xy[k]}, device_id_type=MESH,
            ).start()

    def to_sib(block, cols, n):
        return pltpu.make_async_remote_copy(
            src_ref=C.at[block, :, cols], dst_ref=C.at[block, :, cols],
            send_sem=cs_sem, recv_sem=sib_sem.at[n],
            device_id={"band": sib}, device_id_type=MESH,
        )

    events = ((1, 1), (-1, 1), (1, 2), (-1, 2), (1, 3), (-1, 3), (1, 4))
    last = {1: 4, -1: 3}

    def block_of(side, s, base=None):
        base = b if base is None else base
        return (base + 2 * side * s * dirn + 32) % 16

    def distance(side, s):
        return (side * s * dirn + 8) % 8 - 1

    def ring_event(n):
        side, s = events[n]
        block = block_of(side, s)
        ring(block, 0, n).wait_recv()
        if s < last[side]:
            ring(block, -2 * side * dirn, events.index((side, s + 1))).start()
        spread(block, distance(side, s))
        to_sib(block, mine, n).start()

    def xy_event(n):
        side, s = events[n]
        block = block_of(side, s)
        whole = C.at[block, :, theirs]
        pltpu.make_async_copy(whole, whole, xy_sem.at[distance(side, s)]).wait()
        to_sib(block, theirs, n).start()

    def sib_event(n):
        side, s = events[n]
        to_sib(block_of(side, s, sib), pl.ds(0, KALL), n).wait_recv()

    ring(b, -2 * dirn, 0).start()

    @pl.when(has_send)
    def _():
        mask_copy.start()

    for j in range(NCH):
        count = CH if j < NCH - 1 else KD - CH * (NCH - 1)
        for i in range(ROWS):
            load(j, i).wait()
            v = wrap(raw[i, pl.ds(j * CH, count), :])
            if count < CH:
                v = jnp.concatenate([v, jnp.zeros((CH - count, LP), F32)], axis=0)
            f[3 + i, pl.ds(j * CH, CH), :] = v
            if i > 0:
                hs[i - 1, pl.ds(j * CH, CH), :] = v.astype(BF16)

        @pl.when(has_send)
        def _():
            halo(j).start()

    ring(b, 2 * dirn, 1).start()
    to_sib(b, pl.ds(0, KALL), 7).start()

    shape = (KP, 128)
    comp = (row_iota(shape) + c * KD).astype(F32)
    direction = jnp.floor((comp + 0.5) * (1.0 / FREQS))
    picked = lane_iota(shape).astype(F32) == comp - FREQS * direction
    speeds = jnp.concatenate([gc[...], jnp.zeros((1, 128 - FREQS), F32)], axis=1)
    speed = jnp.sum(jnp.where(picked, speeds, 0.0), axis=1, keepdims=True)
    speed = jnp.where(row_iota(shape) < KD, speed, 0.0)
    theta = 2.0 * math.pi / DIRS * direction
    cosd, sind = jnp.cos(theta), jnp.sin(theta)
    coef[8] = cosd
    coef[9] = sind
    coef[7] = jnp.abs(speed * sind)
    along = jnp.abs(speed * cosd)
    plane = row_iota((8, 128))
    row = (b * ROWS + jnp.where(up, plane - 3, 6 - plane)).astype(F32)
    inverse = 1.0 / jnp.cos((first_lat + 0.25 * (row + 0.5)) * (math.pi / 180.0))
    for p in range(7):
        coef[p] = along * inverse[p : p + 1]

    def wide(v, n):
        return jnp.concatenate([v] * n, axis=1)

    def advect(rows, shift):
        cols = [wide(coef[p, rows, :], LP // 128) for p in range(8)]
        for s in range(3):
            for p in range(6, s, -1):
                v = f[p, rows, :]
                moved = v - cols[p] * (v - pltpu.roll(v, shift, 1)) - cols[7] * (v - f[p - 1, rows, :])
                f[p, rows, :] = moved * (mask_h[p - 1] if p < 3 else aux[p - 3])

    eacc[...] = jnp.zeros_like(eacc)

    @pl.when(has_recv)
    def _():
        mask_copy.wait_recv()
        for p in range(2):
            mask_h[p] = jnp.broadcast_to(mh[p], (8, LP))

    @pl.when(jnp.logical_not(has_recv))
    def _():
        mask_h[...] = jnp.zeros_like(mask_h)

    @pl.loop(0, NCH)
    def _(j):
        rows = rows_at(j)

        @pl.when(has_recv)
        def _():
            halo(j).wait_recv()
            for p in range(3):
                f[p, rows, :] = hr[p, rows, :].astype(F32)

        @pl.when(jnp.logical_not(has_recv))
        def _():
            for p in range(3):
                f[p, rows, :] = jnp.zeros((CH, LP), F32)

        @pl.when(west)
        def _():
            for h in range(2):
                advect(pl.ds(pl.multiple_of(j * CH + 8 * h, 8), 8), 1)

        @pl.when(jnp.logical_not(west))
        def _():
            for h in range(2):
                advect(pl.ds(pl.multiple_of(j * CH + 8 * h, 8), 8), LP - 1)

        for i in range(ROWS):
            for q in range(4):
                lanes = pl.ds(q * QW, QW)
                v = f[3 + i, rows, lanes]
                eacc[i, :, lanes] = eacc[i, :, lanes] + v[:8] + v[8:]
                stage[4 * row_of(i) + q, rows, :] = (v * v).astype(BF16)

        @pl.when(j == NCH - 1)
        def _():
            at = row_iota((CH, QW))
            for i in range(ROWS):
                for q in range(4):
                    lanes = pl.ds(q * QW, QW)
                    total = jnp.sum(eacc[i, :, lanes], axis=0, keepdims=True)
                    hi = total.astype(BF16).astype(F32)
                    mid = (total - hi).astype(BF16).astype(F32)
                    lo = total - hi - mid
                    sq = stage[4 * row_of(i) + q, rows, :].astype(F32)
                    sq = jnp.where(at == 12, hi, jnp.where(at == 13, mid, jnp.where(at == 14, lo, sq)))
                    stage[4 * row_of(i) + q, rows, :] = sq.astype(BF16)

        place = pl.ds(pl.multiple_of(c * KP + j * CH, CH), CH)

        @pl.loop(1, NB)
        def _(n):
            to = (c + n) % 16
            pltpu.make_async_remote_copy(
                src_ref=stage.at[to, rows, :], dst_ref=S.at[place, :],
                send_sem=ss_sem, recv_sem=sr_sem,
                device_id={"comp": to}, device_id_type=MESH,
            ).start()

        @pl.when(j == 2)
        def _():
            ring_event(0)

        @pl.when(j == 3)
        def _():
            ring_event(1)

        @pl.when(j == 4)
        def _():
            ring_event(2)
            xy_event(0)
            xy_event(1)

        @pl.when(j == 5)
        def _():
            ring_event(3)

    S[pl.ds(pl.multiple_of(c * KP, CH), KP), :] = stage[c]
    xy_event(2)
    xy_event(3)
    ring_event(4)
    for n in (7, 0, 1, 2, 3):
        if n == 7:
            to_sib(sib, pl.ds(0, KALL), 7).wait_recv()
        else:
            sib_event(n)
    rest = S.at[pl.ds(0, (NB - 1) * KP), :]
    pltpu.make_async_copy(rest, rest, sr_sem).wait()

    def back(to):
        return pltpu.make_async_remote_copy(
            src_ref=tst.at[to], dst_ref=trv.at[c], send_sem=ts_sem, recv_sem=tr_sem.at[c],
            device_id={"comp": to}, device_id_type=MESH,
        )

    def code(t):
        at = row_iota((KP, QW))
        mean = t[KD : KD + 1] * (1.0 / COMPS)
        t = jnp.maximum(t, -6.0)
        top = jnp.max(jnp.where(at < KD, jnp.abs(t), 0.0), axis=0, keepdims=True)
        power = jnp.ceil(jnp.log2(jnp.maximum(top, 1e-12)) + 0.01)
        scaled = t * (32000.0 * jnp.exp2(-power))
        hi = jnp.floor(mean * 16000.0)
        lo = (mean * 16000.0 - hi) * 32000.0
        scaled = jnp.where(at < KD, scaled, jnp.where(at == KD, power, jnp.where(at == KD + 1, hi, lo)))
        return jnp.round(scaled).astype(jnp.int32).astype(jnp.int16)

    def multiply(chip):
        lhs = C[pl.ds(chip * 2, 2)].reshape(2 * KP, KALL)
        t = jnp.dot(lhs, S[...], preferred_element_type=F32)
        for k in range(2):
            to = chip * 2 + k
            tst[to] = code(t[k * KP : (k + 1) * KP])

            @pl.when(to != c)
            def _():
                back(to).start()

    @pl.loop(0, 5)
    def _(n):
        multiply((z + (n + c) % 5 + 6) % 8)

        @pl.when(n == 0)
        def _():
            ring_event(5)

        @pl.when(n == 1)
        def _():
            ring_event(6)

        @pl.when(n == 2)
        def _():
            xy_event(4)
            xy_event(5)

        @pl.when(n == 3)
        def _():
            xy_event(6)

    for n in (4, 5, 6):
        sib_event(n)

    @pl.loop(0, 3)
    def _(n):
        multiply((z + (n + c) % 3 + 3) % 8)

    trv[c] = tst[c]

    def finish(i, q, width):
        r = row_of(i)
        o = 4 * r + q
        lanes = pl.ds(pl.multiple_of(q * QW, 128), QW)
        final_lanes = pl.ds(pl.multiple_of(q * QW, 128), width)

        @pl.when(o != c)
        def _():
            pltpu.make_async_copy(tst.at[o], trv.at[o], tr_sem.at[o]).wait()

        info = trv[o, pl.ds(KP - CH, CH), :].astype(jnp.int32).astype(F32)[8:]
        scale = jnp.broadcast_to(jnp.exp2(info)[4:5] * (step_time / 32000.0), (8, QW))
        energy = info[5:6] + info[6:7] * (1.0 / 32000.0)
        energy = jnp.broadcast_to(energy * (step_time * damping / 16000.0), (8, QW))
        mask = aux[i, :, lanes]
        cosw = aux[4 + i, :, lanes] * (step_time * wind_gain)
        sinw = aux[8 + i, :, lanes] * (step_time * wind_gain)
        for j in range(NCH):
            t = trv[o, pl.ds(j * CH, CH), :].astype(jnp.int32).astype(F32)
            for h in range(2):
                rows = pl.ds(j * CH + 8 * h, 8)
                v = f[3 + i, rows, lanes]
                facing = wide(coef[8, rows, :], 3) * cosw + wide(coef[9, rows, :], 3) * sinw
                new = v + (jnp.maximum(facing, 0.0) - energy) * v + t[8 * h : 8 * h + 8] * scale
                new = jnp.maximum(new, 0.0) * mask
                count = min(8, KD - (j * CH + 8 * h))
                raw[i, pl.ds(j * CH + 8 * h, count), final_lanes] = new[:count, :width]

    def result(i):
        return pltpu.make_async_copy(raw.at[i], out.at[:, row_of(i), :], out_sem.at[i])

    @pl.loop(0, ROWS)
    def _(i):
        @pl.loop(0, 3)
        def _(q):
            finish(i, q, QW)

        finish(i, 3, LON - 3 * QW)
        result(i).start()

    @pl.when(has_send)
    def _():
        mask_copy.wait_send()
        pltpu.make_async_copy(hs, hs, hs_sem).wait()

    sent = C.at[pl.ds(0, 15)]
    pltpu.make_async_copy(sent, sent, cs_sem).wait()
    pltpu.make_async_copy(rest, rest, ss_sem).wait()
    tsent = tst.at[pl.ds(0, 15)]
    pltpu.make_async_copy(tsent, tsent, ts_sem).wait()
    for i in range(ROWS):
        result(i).wait()


def body(spectrum, group_courant, coupling, wind_dir, sea_mask, owner_cells, owner_counts):
    vmem = pl.BlockSpec(memory_space=pltpu.VMEM)
    hbm = pl.BlockSpec(memory_space=pl.ANY)
    dma = pltpu.SemaphoreType.DMA
    return pl.pallas_call(
        kernel,
        out_shape=jax.ShapeDtypeStruct((KD, ROWS, LON), F32),
        in_specs=[hbm, vmem, vmem, vmem, vmem],
        out_specs=hbm,
        scratch_shapes=[
            pltpu.VMEM((ROWS, KD, LON), F32),
            pltpu.VMEM((7, KP, LP), F32),
            pltpu.VMEM((3, KP, LP), BF16),
            pltpu.VMEM((3, KP, LP), BF16),
            pltpu.VMEM((10, KP, 128), F32),
            pltpu.VMEM((12, 8, LP), F32),
            pltpu.VMEM((ROWS, 1, LP), F32),
            pltpu.VMEM((2, 1, LP), F32),
            pltpu.VMEM((2, 8, LP), F32),
            pltpu.VMEM((NB, KP, QW), BF16),
            pltpu.VMEM((KALL, QW), BF16),
            pltpu.VMEM((NB, KP, KALL), BF16),
            pltpu.VMEM((NB, KP, QW), jnp.int16),
            pltpu.VMEM((NB, KP, QW), jnp.int16),
            pltpu.VMEM((ROWS, 8, LP), F32),
            dma((NCH, ROWS)), dma, dma((NCH,)), dma, dma, dma, dma, dma, dma((NB,)),
            dma, dma((7,)), dma((7,)), dma((8,)), dma((ROWS,)),
        ],
        compiler_params=pltpu.CompilerParams(
            collective_id=0, has_side_effects=True, vmem_limit_bytes=56 * 2**20
        ),
        cost_estimate=pl.CostEstimate(
            flops=2 * KALL * KALL * QW, bytes_accessed=12 * 2**20, transcendentals=0
        ),
    )(spectrum, group_courant.reshape(1, FREQS), coupling, wind_dir, sea_mask)


def solution(mesh):
    return jax.shard_map(
        body,
        mesh=mesh,
        in_specs=(
            P("comp", "band", None),
            P(),
            P("band", None),
            P("band", None),
            P("band", None),
            P(("band", "comp"), None),
            P(("band", "comp")),
        ),
        out_specs=P("comp", "band", None),
        check_vma=False,
    )
```

```python
import math

import jax
import jax.numpy as jnp
from jax import lax
from jax.experimental import pallas as pl
from jax.experimental.pallas import tpu as pltpu
from jax.sharding import PartitionSpec as P

DIRS = 36
FREQS = 48
COMPS = 1728
LON = 1440
ROWS = 4
NB = 16
KD = COMPS // NB
KP = 112
LP = 1536
KALL = NB * KP
QW = LP // 4
HALF = KALL // 2
CH = 16
NCH = KP // CH

first_lat = 30.0
step_time = 0.5
wind_gain = 0.6
damping = 0.4

LAST = {1: 4, -1: 3}
AT_START = [("start", 1, 1), ("start", -1, 1)]
DURING = {
    1: [("ring", 1, 1)],
    2: [("ring", -1, 1)],
    3: [("ring", 1, 2), ("xy", 1, 1), ("xy", -1, 1)],
    5: [("ring", -1, 2), ("ring", 1, 3)],
}
BEFORE_S = [("xy", 1, 2), ("xy", -1, 2), ("ring", 1, 4), ("ring", -1, 3), ("xy", 1, 4), ("xy", 1, 3), ("xy", -1, 3)]
AFTER_S = [("sib", 1, 1), ("sib", -1, 1), ("sib", 1, 2), ("sib", -1, 2),("sib", 1, 3), ("sib", -1, 3), ("sib", 1, 4)]
NEAR = (0, 1, 2, 3, 4, 5, 6, 7)
IN_NEAR = {}
AFTER_NEAR = []
FAR = ()

MESH = pl.DeviceIdType.MESH
F32 = jnp.float32
BF16 = jnp.bfloat16


def lane_iota(shape):
    return lax.broadcasted_iota(jnp.int32, shape, 1)


def row_iota(shape):
    return lax.broadcasted_iota(jnp.int32, shape, 0)


def kernel(
    spec, gc, coup, wind, sea, out,
    raw, f, hs, hr, coef, aux, mrow, mh, mask_h, stage, S, C, tst, trv, eacc,
    load_sem, hs_sem, hr_sem, ms_sem, mr_sem, ss_sem, sr_sem, ts_sem, tr_sem,
    cs_sem, ring_sem, xy_sem, sib_sem, out_sem,
):
    b = lax.axis_index("band")
    c = lax.axis_index("comp")
    z, core = b // 2, b % 2
    y, x = c // 4, c % 4
    up = c < 8
    dirn = jnp.where(up, 1, -1)
    west = jnp.logical_or(c < 4, c >= 12)
    has_send = jnp.where(up, b < 15, b > 0)
    has_recv = jnp.where(up, b > 0, b < 15)
    to_band = (b + dirn + 16) % 16
    sib = b + 1 - 2 * core
    half = (x + y) % 2

    def row_of(i):
        return jnp.where(up, i, 3 - i)

    def rows_at(j, count=CH):
        return pl.ds(pl.multiple_of(j * CH, CH), count)

    def load(j, i):
        count = CH if j < NCH - 1 else KD - CH * (NCH - 1)
        return pltpu.make_async_copy(
            spec.at[pl.ds(j * CH, count), row_of(i), :],
            raw.at[i, pl.ds(j * CH, count), :],
            load_sem.at[j, i],
        )

    for j in range(NCH):
        for i in range(ROWS):
            load(j, i).start()

    barrier = pltpu.get_barrier_semaphore()

    @pl.loop(1, NB)
    def _(n):
        pl.semaphore_signal(barrier, inc=1, device_id={"comp": (c + n) % 16}, device_id_type=MESH)

    for n in (1, 2, 14, 15):
        pl.semaphore_signal(barrier, inc=1, device_id={"band": (b + n) % 16}, device_id_type=MESH)

    def pad_cols(v):
        n = v.shape[0]
        parts = []
        for s in range(NB):
            parts.append(v[:, s * KD : (s + 1) * KD])
            parts.append(jnp.zeros((n, KP - KD), F32))
        return jnp.concatenate(parts, axis=1)

    @pl.loop(0, NCH - 1)
    def _(g):
        C[b, rows_at(g), :] = pad_cols(coup[rows_at(g), :].astype(F32)).astype(BF16)

    tail = pad_cols(coup[KD - 12 :, :].astype(F32))
    tail = jnp.concatenate([tail, jnp.zeros((4, KALL), F32)], axis=0)
    spot = lane_iota((CH, KALL)) % KP
    ones = jnp.logical_and(spot >= KD, spot < KD + 3)
    ones = jnp.logical_and(ones, row_iota((CH, KALL)) == 12)
    C[b, pl.ds(KP - CH, CH), :] = jnp.where(ones, 1.0, tail).astype(BF16)

    def wrap(v):
        return jnp.concatenate([v, v[:, :48], v[:, LON - 48 :]], axis=1)

    seas = wrap(sea[...].astype(F32))
    angle = 2.0 * math.pi / DIRS * wind[...].astype(F32)
    cosw, sinw = wrap(jnp.cos(angle)), wrap(jnp.sin(angle))
    for r in range(ROWS):
        for k, v in enumerate((seas, cosw, sinw)):
            aux[4 * k + row_of(r)] = jnp.broadcast_to(v[r : r + 1], (8, LP))
        mrow[row_of(r)] = seas[r : r + 1]

    pl.semaphore_wait(barrier, NB - 1 + 4)

    mask_copy = pltpu.make_async_remote_copy(
        src_ref=mrow.at[pl.ds(2, 2)], dst_ref=mh, send_sem=ms_sem, recv_sem=mr_sem,
        device_id={"band": to_band}, device_id_type=MESH,
    )

    def halo(j):
        rows = rows_at(j)
        return pltpu.make_async_remote_copy(
            src_ref=hs.at[:, rows, :], dst_ref=hr.at[:, rows, :],
            send_sem=hs_sem, recv_sem=hr_sem.at[j],
            device_id={"band": to_band}, device_id_type=MESH,
        )

    mine = pl.ds(pl.multiple_of(half * HALF, 128), HALF)
    theirs = pl.ds(pl.multiple_of((1 - half) * HALF, 128), HALF)

    pieces = ((0, 64), (64, 48))

    def ring(block, step, n, k):
        part = C.at[block, pl.ds(*pieces[k]), mine]
        return pltpu.make_async_remote_copy(
            src_ref=part, dst_ref=part, send_sem=cs_sem, recv_sem=ring_sem.at[n, k],
            device_id={"band": (b + step + 32) % 16}, device_id_type=MESH,
        )

    xy = (
        y * 4 + (x + 1) % 4,
        y * 4 + (x + 3) % 4,
        ((y + 1) % 4) * 4 + x,
        ((y + 3) % 4) * 4 + x,
    )

    def spread(block, at, k):
        for m, (lo, cnt) in enumerate((((0, 32), (32, 32)), ((64, 32), (96, 16)))[k]):
            piece = C.at[block, pl.ds(lo, cnt), mine]
            pltpu.make_async_remote_copy(
                src_ref=piece, dst_ref=piece, send_sem=cs_sem, recv_sem=xy_sem.at[at],
                device_id={"comp": xy[2 * k + m]}, device_id_type=MESH,
            ).start()

    def to_sib(block, n, rows=pl.ds(0, KP), cols=pl.ds(0, KALL)):
        part = C.at[block, rows, cols]
        return pltpu.make_async_remote_copy(
            src_ref=part, dst_ref=part, send_sem=cs_sem, recv_sem=sib_sem.at[n],
            device_id={"band": sib}, device_id_type=MESH,
        )

    events = [(1, s) for s in range(1, LAST[1] + 1)] + [(-1, s) for s in range(1, LAST[-1] + 1)]

    def block_of(side, s, base=None):
        base = b if base is None else base
        return (base + 2 * side * s * dirn + 32) % 16

    def distance(side, s):
        return (side * s * dirn + 8) % 8 - 1

    def ring_start(side, s, block):
        for k in range(2):
            ring(block, -2 * side * dirn, events.index((side, s)), k).start()

    def ring_event(side, s):
        n = events.index((side, s))
        block = block_of(side, s)
        for k in range(2):
            ring(block, 0, n, k).wait_recv()
            if s < LAST[side]:
                ring(block, -2 * side * dirn, events.index((side, s + 1)), k).start()
            spread(block, distance(side, s), k)
            to_sib(block, n, pl.ds(*pieces[k]), mine).start()

    def xy_event(side, s):
        n = events.index((side, s))
        block = block_of(side, s)
        whole = C.at[block, :, theirs]
        pltpu.make_async_copy(whole, whole, xy_sem.at[distance(side, s)]).wait()
        to_sib(block, n, cols=theirs).start()

    def sib_event(side, s):
        to_sib(block_of(side, s, sib), events.index((side, s))).wait_recv()

    def run(steps):
        for kind, side, s in steps:
            if kind == "start":
                ring_start(side, 1, b)
            else:
                {"ring": ring_event, "xy": xy_event, "sib": sib_event}[kind](side, s)

    run(AT_START)

    @pl.when(has_send)
    def _():
        mask_copy.start()

    for j in range(NCH):
        count = CH if j < NCH - 1 else KD - CH * (NCH - 1)
        for i in range(ROWS):
            load(j, i).wait()
            v = wrap(raw[i, pl.ds(j * CH, count), :])
            if count < CH:
                v = jnp.concatenate([v, jnp.zeros((CH - count, LP), F32)], axis=0)
            f[3 + i, pl.ds(j * CH, CH), :] = v
            if i > 0:
                hs[i - 1, pl.ds(j * CH, CH), :] = v.astype(BF16)

        @pl.when(has_send)
        def _():
            halo(j).start()

    to_sib(b, 7).start()

    shape = (KP, 128)
    comp = (row_iota(shape) + c * KD).astype(F32)
    direction = jnp.floor((comp + 0.5) * (1.0 / FREQS))
    picked = lane_iota(shape).astype(F32) == comp - FREQS * direction
    speeds = jnp.concatenate([gc[...], jnp.zeros((1, 128 - FREQS), F32)], axis=1)
    speed = jnp.sum(jnp.where(picked, speeds, 0.0), axis=1, keepdims=True)
    speed = jnp.where(row_iota(shape) < KD, speed, 0.0)
    theta = 2.0 * math.pi / DIRS * direction
    cosd, sind = jnp.cos(theta), jnp.sin(theta)
    coef[8] = cosd
    coef[9] = sind
    coef[7] = jnp.abs(speed * sind)
    along = jnp.abs(speed * cosd)
    plane = row_iota((8, 128))
    row = (b * ROWS + jnp.where(up, plane - 3, 6 - plane)).astype(F32)
    inverse = 1.0 / jnp.cos((first_lat + 0.25 * (row + 0.5)) * (math.pi / 180.0))
    for p in range(7):
        coef[p] = along * inverse[p : p + 1]

    def wide(v, n):
        return jnp.concatenate([v] * n, axis=1)

    def advect(rows, shift):
        cols = [wide(coef[p, rows, :], LP // 128) for p in range(8)]
        for s in range(3):
            for p in range(6, s, -1):
                v = f[p, rows, :]
                moved = v - cols[p] * (v - pltpu.roll(v, shift, 1)) - cols[7] * (v - f[p - 1, rows, :])
                f[p, rows, :] = moved * (mask_h[p - 1] if p < 3 else aux[p - 3])

    eacc[...] = jnp.zeros_like(eacc)

    @pl.when(has_recv)
    def _():
        mask_copy.wait_recv()
        for p in range(2):
            mask_h[p] = jnp.broadcast_to(mh[p], (8, LP))

    @pl.when(jnp.logical_not(has_recv))
    def _():
        mask_h[...] = jnp.zeros_like(mask_h)

    @pl.loop(0, NCH)
    def _(j):
        rows = rows_at(j)

        @pl.when(has_recv)
        def _():
            halo(j).wait_recv()
            for p in range(3):
                f[p, rows, :] = hr[p, rows, :].astype(F32)

        @pl.when(jnp.logical_not(has_recv))
        def _():
            for p in range(3):
                f[p, rows, :] = jnp.zeros((CH, LP), F32)

        @pl.when(west)
        def _():
            for h in range(2):
                advect(pl.ds(pl.multiple_of(j * CH + 8 * h, 8), 8), 1)

        @pl.when(jnp.logical_not(west))
        def _():
            for h in range(2):
                advect(pl.ds(pl.multiple_of(j * CH + 8 * h, 8), 8), LP - 1)

        for i in range(ROWS):
            for q in range(4):
                lanes = pl.ds(q * QW, QW)
                v = f[3 + i, rows, lanes]
                eacc[i, :, lanes] = eacc[i, :, lanes] + v[:8] + v[8:]
                stage[4 * row_of(i) + q, rows, :] = (v * v).astype(BF16)

        @pl.when(j == NCH - 1)
        def _():
            at = row_iota((CH, QW))
            for i in range(ROWS):
                for q in range(4):
                    lanes = pl.ds(q * QW, QW)
                    total = jnp.sum(eacc[i, :, lanes], axis=0, keepdims=True)
                    hi = total.astype(BF16).astype(F32)
                    mid = (total - hi).astype(BF16).astype(F32)
                    lo = total - hi - mid
                    sq = stage[4 * row_of(i) + q, rows, :].astype(F32)
                    sq = jnp.where(at == 12, hi, jnp.where(at == 13, mid, jnp.where(at == 14, lo, sq)))
                    stage[4 * row_of(i) + q, rows, :] = sq.astype(BF16)

        place = pl.ds(pl.multiple_of(c * KP + j * CH, CH), CH)

        @pl.loop(1, NB)
        def _(n):
            to = (c + n) % 16
            pltpu.make_async_remote_copy(
                src_ref=stage.at[to, rows, :], dst_ref=S.at[place, :],
                send_sem=ss_sem, recv_sem=sr_sem,
                device_id={"comp": to}, device_id_type=MESH,
            ).start()

        for at, steps in DURING.items():
            @pl.when(j == at)
            def _(steps=steps):
                run(steps)

    S[pl.ds(pl.multiple_of(c * KP, CH), KP), :] = stage[c]
    run(BEFORE_S)
    to_sib(sib, 7).wait_recv()
    rest = S.at[pl.ds(0, (NB - 1) * KP), :]
    pltpu.make_async_copy(rest, rest, sr_sem).wait()
    run(AFTER_S)

    def back(to):
        return pltpu.make_async_remote_copy(
            src_ref=tst.at[to], dst_ref=trv.at[c], send_sem=ts_sem, recv_sem=tr_sem.at[c],
            device_id={"comp": to}, device_id_type=MESH,
        )

    def code(t):
        at = row_iota((KP, QW))
        mean = t[KD : KD + 1] * (1.0 / COMPS)
        t = jnp.maximum(t, -6.0)
        top = jnp.max(jnp.where(at < KD, jnp.abs(t), 0.0), axis=0, keepdims=True)
        power = jnp.ceil(jnp.log2(jnp.maximum(top, 1e-12)) + 0.01)
        scaled = t * (32000.0 * jnp.exp2(-power))
        hi = jnp.floor(mean * 16000.0)
        lo = (mean * 16000.0 - hi) * 32000.0
        scaled = jnp.where(at < KD, scaled, jnp.where(at == KD, power, jnp.where(at == KD + 1, hi, lo)))
        return jnp.round(scaled).astype(jnp.int32).astype(jnp.int16)

    def multiply(chip):
        lhs = C[pl.ds(chip * 2, 2)].reshape(2 * KP, KALL)
        t = jnp.dot(lhs, S[...], preferred_element_type=F32)
        for k in range(2):
            to = chip * 2 + k
            tst[to] = code(t[k * KP : (k + 1) * KP])

            @pl.when(to != c)
            def _():
                back(to).start()

    def pick(group, n):
        m = (n + c) % len(group)
        away = group[0]
        for k in range(1, len(group)):
            away = jnp.where(m == k, group[k], away)
        return (z + away) % 8

    @pl.loop(0, len(NEAR))
    def _(n):
        multiply(pick(NEAR, n))
        for at, steps in IN_NEAR.items():
            @pl.when(n == at)
            def _(steps=steps):
                run(steps)

    run(AFTER_NEAR)
    if FAR:

        @pl.loop(0, len(FAR))
        def _(n):
            multiply(pick(FAR, n))

    trv[c] = tst[c]

    def finish(i, q, width):
        r = row_of(i)
        o = 4 * r + q
        lanes = pl.ds(pl.multiple_of(q * QW, 128), QW)
        final_lanes = pl.ds(pl.multiple_of(q * QW, 128), width)

        @pl.when(o != c)
        def _():
            pltpu.make_async_copy(tst.at[o], trv.at[o], tr_sem.at[o]).wait()

        info = trv[o, pl.ds(KP - CH, CH), :].astype(jnp.int32).astype(F32)[8:]
        scale = jnp.broadcast_to(jnp.exp2(info)[4:5] * (step_time / 32000.0), (8, QW))
        energy = info[5:6] + info[6:7] * (1.0 / 32000.0)
        energy = jnp.broadcast_to(energy * (step_time * damping / 16000.0), (8, QW))
        mask = aux[i, :, lanes]
        cosw = aux[4 + i, :, lanes] * (step_time * wind_gain)
        sinw = aux[8 + i, :, lanes] * (step_time * wind_gain)
        for j in range(NCH):
            t = trv[o, pl.ds(j * CH, CH), :].astype(jnp.int32).astype(F32)
            for h in range(2):
                rows = pl.ds(j * CH + 8 * h, 8)
                v = f[3 + i, rows, lanes]
                facing = wide(coef[8, rows, :], 3) * cosw + wide(coef[9, rows, :], 3) * sinw
                new = v + (jnp.maximum(facing, 0.0) - energy) * v + t[8 * h : 8 * h + 8] * scale
                new = jnp.maximum(new, 0.0) * mask
                count = min(8, KD - (j * CH + 8 * h))
                raw[i, pl.ds(j * CH + 8 * h, count), final_lanes] = new[:count, :width]

    def result(i):
        return pltpu.make_async_copy(raw.at[i], out.at[:, row_of(i), :], out_sem.at[i])

    @pl.loop(0, ROWS)
    def _(i):
        @pl.loop(0, 3)
        def _(q):
            finish(i, q, QW)

        finish(i, 3, LON - 3 * QW)
        result(i).start()

    @pl.when(has_send)
    def _():
        mask_copy.wait_send()
        pltpu.make_async_copy(hs, hs, hs_sem).wait()

    sent = C.at[pl.ds(0, 15)]
    pltpu.make_async_copy(sent, sent, cs_sem).wait()
    pltpu.make_async_copy(rest, rest, ss_sem).wait()
    tsent = tst.at[pl.ds(0, 15)]
    pltpu.make_async_copy(tsent, tsent, ts_sem).wait()
    for i in range(ROWS):
        result(i).wait()


def body(spectrum, group_courant, coupling, wind_dir, sea_mask, owner_cells, owner_counts):
    vmem = pl.BlockSpec(memory_space=pltpu.VMEM)
    hbm = pl.BlockSpec(memory_space=pl.ANY)
    dma = pltpu.SemaphoreType.DMA
    return pl.pallas_call(
        kernel,
        out_shape=jax.ShapeDtypeStruct((KD, ROWS, LON), F32),
        in_specs=[hbm, vmem, vmem, vmem, vmem],
        out_specs=hbm,
        scratch_shapes=[
            pltpu.VMEM((ROWS, KD, LON), F32),
            pltpu.VMEM((7, KP, LP), F32),
            pltpu.VMEM((3, KP, LP), BF16),
            pltpu.VMEM((3, KP, LP), BF16),
            pltpu.VMEM((10, KP, 128), F32),
            pltpu.VMEM((12, 8, LP), F32),
            pltpu.VMEM((ROWS, 1, LP), F32),
            pltpu.VMEM((2, 1, LP), F32),
            pltpu.VMEM((2, 8, LP), F32),
            pltpu.VMEM((NB, KP, QW), BF16),
            pltpu.VMEM((KALL, QW), BF16),
            pltpu.VMEM((NB, KP, KALL), BF16),
            pltpu.VMEM((NB, KP, QW), jnp.int16),
            pltpu.VMEM((NB, KP, QW), jnp.int16),
            pltpu.VMEM((ROWS, 8, LP), F32),
            dma((NCH, ROWS)), dma, dma((NCH,)), dma, dma, dma, dma, dma, dma((NB,)),
            dma, dma((7, 2)), dma((7,)), dma((8,)), dma((ROWS,)),
        ],
        compiler_params=pltpu.CompilerParams(
            collective_id=0, has_side_effects=True, vmem_limit_bytes=56 * 2**20
        ),
        cost_estimate=pl.CostEstimate(
            flops=2 * KALL * KALL * QW, bytes_accessed=12 * 2**20, transcendentals=0
        ),
    )(spectrum, group_courant.reshape(1, FREQS), coupling, wind_dir, sea_mask)


def solution(mesh):
    return jax.shard_map(
        body,
        mesh=mesh,
        in_specs=(
            P("comp", "band", None),
            P(),
            P("band", None),
            P("band", None),
            P("band", None),
            P(("band", "comp"), None),
            P(("band", "comp")),
        ),
        out_specs=P("comp", "band", None),
        check_vma=False,
    )
```

```python
import math

import jax
import jax.numpy as jnp
from jax import lax
from jax.experimental import pallas as pl
from jax.experimental.pallas import tpu as pltpu
from jax.sharding import PartitionSpec as P

DIRS = 36
FREQS = 48
COMPS = 1728
LON = 1440
ROWS = 4
NB = 16
KD = COMPS // NB
KP = 112
LP = 1536
KALL = NB * KP
QW = LP // 4
HALF = KALL // 2
CH = 16
NCH = KP // CH

first_lat = 30.0
step_time = 0.5
wind_gain = 0.6
damping = 0.4

LAST = {1: 4, -1: 3}
AT_START = [("start", 1, 1), ("start", -1, 1)]
DURING = {0: [("ring", 1, 1)], 2: [("ring", 1, 2), ("ring", -1, 1)], 4: [("ring", 1, 3), ("xy", 1, 1), ("xy", -1, 1)], 5: [("ring", -1, 2)], 6: [("ring", 1, 4)]}
BEFORE_S = [("xy", 1, 2), ("xy", -1, 2), ("ring", -1, 3), ("xy", 1, 4), ("xy", 1, 3), ("xy", -1, 3)]
AFTER_S = [("sib", 1, 1), ("sib", -1, 1), ("sib", 1, 2), ("sib", -1, 2),("sib", 1, 3), ("sib", -1, 3), ("sib", 1, 4)]

ORDER = ((1, 0), (3, 1), (0, 1), (2, 0), (1, 1), (3, 0), (2, 1), (0, 0))

MESH = pl.DeviceIdType.MESH
F32 = jnp.float32
BF16 = jnp.bfloat16


def lane_iota(shape):
    return lax.broadcasted_iota(jnp.int32, shape, 1)


def row_iota(shape):
    return lax.broadcasted_iota(jnp.int32, shape, 0)


def sine(v):
    square = v * v
    total = jnp.full_like(v, 1.0 / math.factorial(13))
    for n in (11, 9, 7, 5, 3, 1):
        total = total * square + (-1.0) ** (n // 2) / math.factorial(n)
    return total * v


def cosine_of(step):
    return sine((jnp.abs(step - 18.0) - 9.0) * (2.0 * math.pi / DIRS))


def sine_of(step):
    return cosine_of(jnp.where(step < 9.0, step + 27.0, step - 9.0))


def kernel(
    spec, gc, coup, wind, sea, out,
    raw, f, hs, hr, coef, aux, mrow, mh, mask_h, stage, S, C, tst, trv, eacc,
    load_sem, hs_sem, hr_sem, ms_sem, mr_sem, ss_sem, sr_sem, ts_sem, tr_sem,
    cs_sem, ring_sem, xy_sem, sib_sem, out_sem,
):
    b = lax.axis_index("band")
    c = lax.axis_index("comp")
    z, core = b // 2, b % 2
    y, x = c // 4, c % 4
    up = c < 8
    dirn = jnp.where(up, 1, -1)
    west = jnp.logical_or(c < 4, c >= 12)
    has_send = jnp.where(up, b < 15, b > 0)
    has_recv = jnp.where(up, b > 0, b < 15)
    to_band = (b + dirn + 16) % 16
    sib = b + 1 - 2 * core
    half = (x + y) % 2

    def row_of(i):
        return jnp.where(up, i, 3 - i)

    def rows_at(j, count=CH):
        return pl.ds(pl.multiple_of(j * CH, CH), count)

    def load(j, i):
        count = CH if j < NCH - 1 else KD - CH * (NCH - 1)
        return pltpu.make_async_copy(
            spec.at[pl.ds(j * CH, count), row_of(i), :],
            raw.at[i, pl.ds(j * CH, count), :],
            load_sem.at[j, i],
        )

    for j in range(NCH):
        for i in range(ROWS):
            load(j, i).start()

    barrier = pltpu.get_barrier_semaphore()

    @pl.loop(1, NB)
    def _(n):
        pl.semaphore_signal(barrier, inc=1, device_id={"comp": (c + n) % 16}, device_id_type=MESH)

    for n in (1, 2, 14, 15):
        pl.semaphore_signal(barrier, inc=1, device_id={"band": (b + n) % 16}, device_id_type=MESH)

    def pad_cols(v):
        n = v.shape[0]
        parts = []
        for s in range(NB):
            parts.append(v[:, s * KD : (s + 1) * KD])
            parts.append(jnp.zeros((n, KP - KD), F32))
        return jnp.concatenate(parts, axis=1)

    @pl.loop(0, NCH - 1)
    def _(g):
        C[b, rows_at(g), :] = pad_cols(coup[rows_at(g), :].astype(F32)).astype(BF16)

    tail = pad_cols(coup[KD - 12 :, :].astype(F32))
    tail = jnp.concatenate([tail, jnp.zeros((4, KALL), F32)], axis=0)
    spot = lane_iota((CH, KALL)) % KP
    ones = jnp.logical_and(spot >= KD, spot < KD + 3)
    ones = jnp.logical_and(ones, row_iota((CH, KALL)) == 12)
    C[b, pl.ds(KP - CH, CH), :] = jnp.where(ones, 1.0, tail).astype(BF16)

    def wrap(v):
        return jnp.concatenate([v, v[:, :48], v[:, LON - 48 :]], axis=1)

    seas = wrap(sea[...].astype(F32))
    for r in range(ROWS):
        mrow[row_of(r)] = seas[r : r + 1]

    pl.semaphore_wait(barrier, NB - 1 + 4)

    mask_copy = pltpu.make_async_remote_copy(
        src_ref=mrow.at[pl.ds(2, 2)], dst_ref=mh, send_sem=ms_sem, recv_sem=mr_sem,
        device_id={"band": to_band}, device_id_type=MESH,
    )

    @pl.when(has_send)
    def _():
        mask_copy.start()

    def halo(j):
        rows = rows_at(j)
        return pltpu.make_async_remote_copy(
            src_ref=hs.at[:, rows, :], dst_ref=hr.at[:, rows, :],
            send_sem=hs_sem, recv_sem=hr_sem.at[j],
            device_id={"band": to_band}, device_id_type=MESH,
        )

    mine = pl.ds(pl.multiple_of(half * HALF, 128), HALF)
    theirs = pl.ds(pl.multiple_of((1 - half) * HALF, 128), HALF)

    pieces = ((0, 64), (64, 48))

    def ring(block, step, n, k):
        part = C.at[block, pl.ds(*pieces[k]), mine]
        return pltpu.make_async_remote_copy(
            src_ref=part, dst_ref=part, send_sem=cs_sem, recv_sem=ring_sem.at[n, k],
            device_id={"band": (b + step + 32) % 16}, device_id_type=MESH,
        )

    xy = (
        y * 4 + (x + 1) % 4,
        y * 4 + (x + 3) % 4,
        ((y + 1) % 4) * 4 + x,
        ((y + 3) % 4) * 4 + x,
    )

    def spread(block, at, k):
        for m, (lo, cnt) in enumerate((((0, 32), (32, 32)), ((64, 32), (96, 16)))[k]):
            piece = C.at[block, pl.ds(lo, cnt), mine]
            pltpu.make_async_remote_copy(
                src_ref=piece, dst_ref=piece, send_sem=cs_sem, recv_sem=xy_sem.at[at],
                device_id={"comp": xy[2 * k + m]}, device_id_type=MESH,
            ).start()

    def to_sib(block, n, rows=pl.ds(0, KP), cols=pl.ds(0, KALL)):
        part = C.at[block, rows, cols]
        return pltpu.make_async_remote_copy(
            src_ref=part, dst_ref=part, send_sem=cs_sem, recv_sem=sib_sem.at[n],
            device_id={"band": sib}, device_id_type=MESH,
        )

    events = [(1, s) for s in range(1, LAST[1] + 1)] + [(-1, s) for s in range(1, LAST[-1] + 1)]

    def block_of(side, s, base=None):
        base = b if base is None else base
        return (base + 2 * side * s * dirn + 32) % 16

    def distance(side, s):
        return (side * s * dirn + 8) % 8 - 1

    def ring_start(side, s, block):
        for k in range(2):
            ring(block, -2 * side * dirn, events.index((side, s)), k).start()

    def ring_event(side, s):
        n = events.index((side, s))
        block = block_of(side, s)
        for k in range(2):
            ring(block, 0, n, k).wait_recv()
            if s < LAST[side]:
                ring(block, -2 * side * dirn, events.index((side, s + 1)), k).start()
            spread(block, distance(side, s), k)
            to_sib(block, n, pl.ds(*pieces[k]), mine).start()

    def xy_event(side, s):
        n = events.index((side, s))
        block = block_of(side, s)
        whole = C.at[block, :, theirs]
        pltpu.make_async_copy(whole, whole, xy_sem.at[distance(side, s)]).wait()
        to_sib(block, n, cols=theirs).start()

    def sib_event(side, s):
        to_sib(block_of(side, s, sib), events.index((side, s))).wait_recv()

    def run(steps):
        for kind, side, s in steps:
            if kind == "start":
                ring_start(side, 1, b)
            else:
                {"ring": ring_event, "xy": xy_event, "sib": sib_event}[kind](side, s)

    run(AT_START)

    for j in range(NCH):
        count = CH if j < NCH - 1 else KD - CH * (NCH - 1)
        for i in range(ROWS):
            load(j, i).wait()
            v = wrap(raw[i, pl.ds(j * CH, count), :])
            if count < CH:
                v = jnp.concatenate([v, jnp.zeros((CH - count, LP), F32)], axis=0)
            f[3 + i, pl.ds(j * CH, CH), :] = v
            if i > 0:
                hs[i - 1, pl.ds(j * CH, CH), :] = v.astype(BF16)

        @pl.when(has_send)
        def _():
            halo(j).start()

    to_sib(b, 7).start()

    blowing = wind[...].astype(F32)
    cosw, sinw = wrap(cosine_of(blowing)), wrap(sine_of(blowing))
    for r in range(ROWS):
        for k, v in enumerate((seas, cosw, sinw)):
            aux[4 * k + row_of(r)] = jnp.broadcast_to(v[r : r + 1], (8, LP))

    shape = (KP, 128)
    comp = (row_iota(shape) + c * KD).astype(F32)
    direction = jnp.floor((comp + 0.5) * (1.0 / FREQS))
    picked = lane_iota(shape).astype(F32) == comp - FREQS * direction
    speeds = jnp.concatenate([gc[...], jnp.zeros((1, 128 - FREQS), F32)], axis=1)
    speed = jnp.sum(jnp.where(picked, speeds, 0.0), axis=1, keepdims=True)
    speed = jnp.where(row_iota(shape) < KD, speed, 0.0)
    cosd, sind = cosine_of(direction), sine_of(direction)
    coef[8] = cosd
    coef[9] = sind
    coef[7] = jnp.abs(speed * sind)
    along = jnp.abs(speed * cosd)
    plane = row_iota((8, 128))
    row = (b * ROWS + jnp.where(up, plane - 3, 6 - plane)).astype(F32)
    inverse = 1.0 / sine((90.0 - first_lat - 0.25 * (row + 0.5)) * (math.pi / 180.0))
    for p in range(7):
        coef[p] = along * inverse[p : p + 1]

    def wide(v, n):
        return jnp.concatenate([v] * n, axis=1)

    def pair_of(n):
        away, other = ORDER[0]
        for k in range(1, len(ORDER)):
            away = jnp.where(n == k, ORDER[k][0], away)
            other = jnp.where(n == k, ORDER[k][1], other)
        return ((y + jnp.where(core == 1, 4 - away, away)) % 4) * 2 + (x // 2 + other) % 2

    def advect(rows, shift):
        cols = [wide(coef[p, rows, :], LP // 128) for p in range(8)]
        for s in range(3):
            for p in range(6, s, -1):
                v = f[p, rows, :]
                moved = v - cols[p] * (v - pltpu.roll(v, shift, 1)) - cols[7] * (v - f[p - 1, rows, :])
                f[p, rows, :] = moved * (mask_h[p - 1] if p < 3 else aux[p - 3])

    eacc[...] = jnp.zeros_like(eacc)

    @pl.when(has_recv)
    def _():
        mask_copy.wait_recv()
        for p in range(2):
            mask_h[p] = jnp.broadcast_to(mh[p], (8, LP))

    @pl.when(jnp.logical_not(has_recv))
    def _():
        mask_h[...] = jnp.zeros_like(mask_h)

    @pl.loop(0, NCH)
    def _(j):
        rows = rows_at(j)

        @pl.when(has_recv)
        def _():
            halo(j).wait_recv()
            for p in range(3):
                f[p, rows, :] = hr[p, rows, :].astype(F32)

        @pl.when(jnp.logical_not(has_recv))
        def _():
            for p in range(3):
                f[p, rows, :] = jnp.zeros((CH, LP), F32)

        @pl.when(west)
        def _():
            for h in range(2):
                advect(pl.ds(pl.multiple_of(j * CH + 8 * h, 8), 8), 1)

        @pl.when(jnp.logical_not(west))
        def _():
            for h in range(2):
                advect(pl.ds(pl.multiple_of(j * CH + 8 * h, 8), 8), LP - 1)

        for i in range(ROWS):
            for q in range(4):
                lanes = pl.ds(q * QW, QW)
                v = f[3 + i, rows, lanes]
                eacc[i, :, lanes] = eacc[i, :, lanes] + v[:8] + v[8:]
                stage[4 * row_of(i) + q, rows, :] = (v * v).astype(BF16)

        @pl.when(j == NCH - 1)
        def _():
            at = row_iota((CH, QW))
            for i in range(ROWS):
                for q in range(4):
                    lanes = pl.ds(q * QW, QW)
                    total = jnp.sum(eacc[i, :, lanes], axis=0, keepdims=True)
                    hi = total.astype(BF16).astype(F32)
                    mid = (total - hi).astype(BF16).astype(F32)
                    lo = total - hi - mid
                    sq = stage[4 * row_of(i) + q, rows, :].astype(F32)
                    sq = jnp.where(at == 12, hi, jnp.where(at == 13, mid, jnp.where(at == 14, lo, sq)))
                    stage[4 * row_of(i) + q, rows, :] = sq.astype(BF16)

        place = pl.ds(pl.multiple_of(c * KP + j * CH, CH), CH)

        @pl.loop(0, len(ORDER))
        def _(n):
            for k in range(2):
                to = pair_of(n) * 2 + k

                @pl.when(to != c)
                def _():
                    pltpu.make_async_remote_copy(
                        src_ref=stage.at[to, rows, :], dst_ref=S.at[place, :],
                        send_sem=ss_sem, recv_sem=sr_sem,
                        device_id={"comp": to}, device_id_type=MESH,
                    ).start()

        for at, steps in DURING.items():
            @pl.when(j == at)
            def _(steps=steps):
                run(steps)

    S[pl.ds(pl.multiple_of(c * KP, CH), KP), :] = stage[c]
    run(BEFORE_S)
    to_sib(sib, 7).wait_recv()
    rest = S.at[pl.ds(0, (NB - 1) * KP), :]
    pltpu.make_async_copy(rest, rest, sr_sem).wait()
    run(AFTER_S)

    def back(to):
        return pltpu.make_async_remote_copy(
            src_ref=tst.at[to], dst_ref=trv.at[c], send_sem=ts_sem, recv_sem=tr_sem.at[c],
            device_id={"comp": to}, device_id_type=MESH,
        )

    def code(t):
        at = row_iota((KP, QW))
        mean = t[KD : KD + 1] * (1.0 / COMPS)
        t = jnp.maximum(t, -6.0)
        top = jnp.max(jnp.where(at < KD, jnp.abs(t), 0.0), axis=0, keepdims=True)
        power = jnp.ceil(jnp.log2(jnp.maximum(top, 1e-12)) + 0.01)
        scaled = t * (32000.0 * jnp.exp2(-power))
        hi = jnp.floor(mean * 16000.0)
        lo = (mean * 16000.0 - hi) * 32000.0
        scaled = jnp.where(at < KD, scaled, jnp.where(at == KD, power, jnp.where(at == KD + 1, hi, lo)))
        return jnp.round(scaled).astype(jnp.int32).astype(jnp.int16)

    def multiply(chip):
        lhs = C[pl.ds(chip * 2, 2)].reshape(2 * KP, KALL)
        t = jnp.dot(lhs, S[...], preferred_element_type=F32)
        for k in range(2):
            to = chip * 2 + k
            tst[to] = code(t[k * KP : (k + 1) * KP])

            @pl.when(to != c)
            def _():
                back(to).start()

    @pl.loop(0, len(ORDER))
    def _(n):
        multiply(pair_of(n))

    trv[c] = tst[c]

    def finish(i, q, width):
        r = row_of(i)
        o = 4 * r + q
        lanes = pl.ds(pl.multiple_of(q * QW, 128), QW)
        final_lanes = pl.ds(pl.multiple_of(q * QW, 128), width)

        @pl.when(o != c)
        def _():
            pltpu.make_async_copy(tst.at[o], trv.at[o], tr_sem.at[o]).wait()

        info = trv[o, pl.ds(KP - CH, CH), :].astype(jnp.int32).astype(F32)[8:]
        scale = jnp.broadcast_to(jnp.exp2(info)[4:5] * (step_time / 32000.0), (8, QW))
        energy = info[5:6] + info[6:7] * (1.0 / 32000.0)
        energy = jnp.broadcast_to(energy * (step_time * damping / 16000.0), (8, QW))
        mask = aux[i, :, lanes]
        cosw = aux[4 + i, :, lanes] * (step_time * wind_gain)
        sinw = aux[8 + i, :, lanes] * (step_time * wind_gain)
        for j in range(NCH):
            t = trv[o, pl.ds(j * CH, CH), :].astype(jnp.int32).astype(F32)
            for h in range(2):
                rows = pl.ds(j * CH + 8 * h, 8)
                v = f[3 + i, rows, lanes]
                facing = wide(coef[8, rows, :], 3) * cosw + wide(coef[9, rows, :], 3) * sinw
                new = v + (jnp.maximum(facing, 0.0) - energy) * v + t[8 * h : 8 * h + 8] * scale
                new = jnp.maximum(new, 0.0) * mask
                count = min(8, KD - (j * CH + 8 * h))
                raw[i, pl.ds(j * CH + 8 * h, count), final_lanes] = new[:count, :width]

    def result(i):
        return pltpu.make_async_copy(raw.at[i], out.at[:, row_of(i), :], out_sem.at[i])

    @pl.loop(0, ROWS)
    def _(i):
        @pl.loop(0, 3)
        def _(q):
            finish(i, q, QW)

        finish(i, 3, LON - 3 * QW)
        result(i).start()

    @pl.when(has_send)
    def _():
        mask_copy.wait_send()
        pltpu.make_async_copy(hs, hs, hs_sem).wait()

    sent = C.at[pl.ds(0, 15)]
    pltpu.make_async_copy(sent, sent, cs_sem).wait()
    pltpu.make_async_copy(rest, rest, ss_sem).wait()
    tsent = tst.at[pl.ds(0, 15)]
    pltpu.make_async_copy(tsent, tsent, ts_sem).wait()
    for i in range(ROWS):
        result(i).wait()


def hand_on(src, dst, held, sem, out_sem):
    first, second = [], []
    for k in range(4):
        part = pl.ds(k * (KD // 4), KD // 4)
        first.append(pltpu.make_async_copy(src.at[part], held.at[part], sem.at[k]))
        second.append(pltpu.make_async_copy(held.at[part], dst.at[part], out_sem.at[k]))
    for copy in first:
        copy.start()
    for k in range(4):
        first[k].wait()
        second[k].start()
    for copy in second:
        copy.wait()


def body(spectrum, group_courant, coupling, wind_dir, sea_mask, owner_cells, owner_counts):
    vmem = pl.BlockSpec(memory_space=pltpu.VMEM)
    hbm = pl.BlockSpec(memory_space=pl.ANY)
    dma = pltpu.SemaphoreType.DMA
    staged = pl.pallas_call(
        kernel,
        out_shape=jax.ShapeDtypeStruct((KD, ROWS, LON), F32),
        in_specs=[hbm, vmem, vmem, vmem, vmem],
        out_specs=hbm,
        scratch_shapes=[
            pltpu.VMEM((ROWS, KD, LON), F32),
            pltpu.VMEM((7, KP, LP), F32),
            pltpu.VMEM((3, KP, LP), BF16),
            pltpu.VMEM((3, KP, LP), BF16),
            pltpu.VMEM((10, KP, 128), F32),
            pltpu.VMEM((12, 8, LP), F32),
            pltpu.VMEM((ROWS, 1, LP), F32),
            pltpu.VMEM((2, 1, LP), F32),
            pltpu.VMEM((2, 8, LP), F32),
            pltpu.VMEM((NB, KP, QW), BF16),
            pltpu.VMEM((KALL, QW), BF16),
            pltpu.VMEM((NB, KP, KALL), BF16),
            pltpu.VMEM((NB, KP, QW), jnp.int16),
            pltpu.VMEM((NB, KP, QW), jnp.int16),
            pltpu.VMEM((ROWS, 8, LP), F32),
            dma((NCH, ROWS)), dma, dma((NCH,)), dma, dma, dma, dma, dma, dma((NB,)),
            dma, dma((7, 2)), dma((7,)), dma((8,)), dma((ROWS,)),
        ],
        compiler_params=pltpu.CompilerParams(
            collective_id=0, has_side_effects=True, vmem_limit_bytes=56 * 2**20
        ),
        cost_estimate=pl.CostEstimate(
            flops=2 * KALL * KALL * QW, bytes_accessed=12 * 2**20, transcendentals=0
        ),
    )(spectrum, group_courant.reshape(1, FREQS), coupling, wind_dir, sea_mask)
    return pl.pallas_call(
        hand_on,
        out_shape=jax.ShapeDtypeStruct((KD, ROWS, LON), F32),
        in_specs=[hbm],
        out_specs=hbm,
        scratch_shapes=[pltpu.VMEM((KD, ROWS, LON), F32), dma((4,)), dma((4,))],
    )(staged)


def solution(mesh):
    return jax.shard_map(
        body,
        mesh=mesh,
        in_specs=(
            P("comp", "band", None),
            P(),
            P("band", None),
            P("band", None),
            P("band", None),
            P(("band", "comp"), None),
            P(("band", "comp")),
        ),
        out_specs=P("comp", "band", None),
        check_vma=False,
    )
```

```python
import math

import jax
import jax.numpy as jnp
from jax import lax
from jax.experimental import pallas as pl
from jax.experimental.pallas import tpu as pltpu
from jax.sharding import PartitionSpec as P

DIRS = 36
FREQS = 48
COMPS = 1728
LON = 1440
ROWS = 4
NB = 16
KD = COMPS // NB
KP = 112
LP = 1536
KALL = NB * KP
QW = LP // 4
HALF = KALL // 2
CH = 16
NCH = KP // CH

first_lat = 30.0
step_time = 0.5
wind_gain = 0.6
damping = 0.4

LAST = {1: 4, -1: 3}
AT_START = [("start", 1, 1), ("start", -1, 1)]
DURING = {0: [("ring", 1, 1)], 2: [("ring", 1, 2), ("ring", -1, 1)], 4: [("ring", 1, 3), ("xy", 1, 1), ("xy", -1, 1)], 5: [("ring", -1, 2)], 6: [("ring", 1, 4)]}
BEFORE_S = [("xy", 1, 2), ("xy", -1, 2), ("ring", -1, 3), ("xy", 1, 4), ("xy", 1, 3), ("xy", -1, 3)]
AFTER_S = [("sib", 1, 1), ("sib", -1, 1), ("sib", 1, 2), ("sib", -1, 2),("sib", 1, 3), ("sib", -1, 3), ("sib", 1, 4)]

ORDER = ((1, 0), (3, 1), (0, 1), (2, 0), (1, 1), (3, 0), (2, 1), (0, 0))

MESH = pl.DeviceIdType.MESH
F32 = jnp.float32
BF16 = jnp.bfloat16


def lane_iota(shape):
    return lax.broadcasted_iota(jnp.int32, shape, 1)


def row_iota(shape):
    return lax.broadcasted_iota(jnp.int32, shape, 0)


def sine(v):
    square = v * v
    total = jnp.full_like(v, 1.0 / math.factorial(13))
    for n in (11, 9, 7, 5, 3, 1):
        total = total * square + (-1.0) ** (n // 2) / math.factorial(n)
    return total * v


def cosine_of(step):
    return sine((jnp.abs(step - 18.0) - 9.0) * (2.0 * math.pi / DIRS))


def sine_of(step):
    return cosine_of(jnp.where(step < 9.0, step + 27.0, step - 9.0))


def kernel(
    spec, gc, coup, wind, sea, out,
    raw, f, hs, hr, coef, aux, mrow, mh, mask_h, stage, S, C, tst, trv, eacc,
    load_sem, hs_sem, hr_sem, ms_sem, mr_sem, ss_sem, sr_sem, ts_sem, tr_sem,
    cs_sem, ring_sem, xy_sem, sib_sem, out_sem,
):
    b = lax.axis_index("band")
    c = lax.axis_index("comp")
    z, core = b // 2, b % 2
    y, x = c // 4, c % 4
    up = c < 8
    dirn = jnp.where(up, 1, -1)
    west = jnp.logical_or(c < 4, c >= 12)
    has_send = jnp.where(up, b < 15, b > 0)
    has_recv = jnp.where(up, b > 0, b < 15)
    to_band = (b + dirn + 16) % 16
    sib = b + 1 - 2 * core
    half = (x + y) % 2

    def row_of(i):
        return jnp.where(up, i, 3 - i)

    def rows_at(j, count=CH):
        return pl.ds(pl.multiple_of(j * CH, CH), count)

    def load(j, i):
        count = CH if j < NCH - 1 else KD - CH * (NCH - 1)
        return pltpu.make_async_copy(
            spec.at[pl.ds(j * CH, count), row_of(i), :],
            raw.at[i, pl.ds(j * CH, count), :],
            load_sem.at[j, i],
        )

    for j in range(NCH):
        for i in range(ROWS):
            load(j, i).start()

    barrier = pltpu.get_barrier_semaphore()

    @pl.loop(1, NB)
    def _(n):
        pl.semaphore_signal(barrier, inc=1, device_id={"comp": (c + n) % 16}, device_id_type=MESH)

    for n in (1, 2, 14, 15):
        pl.semaphore_signal(barrier, inc=1, device_id={"band": (b + n) % 16}, device_id_type=MESH)

    def pad_cols(v):
        n = v.shape[0]
        parts = []
        for s in range(NB):
            parts.append(v[:, s * KD : (s + 1) * KD])
            parts.append(jnp.zeros((n, KP - KD), F32))
        return jnp.concatenate(parts, axis=1)

    @pl.loop(0, NCH - 1)
    def _(g):
        C[b, rows_at(g), :] = pad_cols(coup[rows_at(g), :].astype(F32)).astype(BF16)

    tail = pad_cols(coup[KD - 12 :, :].astype(F32))
    tail = jnp.concatenate([tail, jnp.zeros((4, KALL), F32)], axis=0)
    spot = lane_iota((CH, KALL)) % KP
    ones = jnp.logical_and(spot >= KD, spot < KD + 3)
    ones = jnp.logical_and(ones, row_iota((CH, KALL)) == 12)
    C[b, pl.ds(KP - CH, CH), :] = jnp.where(ones, 1.0, tail).astype(BF16)

    def wrap(v):
        return jnp.concatenate([v, v[:, :48], v[:, LON - 48 :]], axis=1)

    seas = wrap(sea[...].astype(F32))
    for r in range(ROWS):
        mrow[row_of(r)] = seas[r : r + 1]

    pl.semaphore_wait(barrier, NB - 1 + 4)

    mask_copy = pltpu.make_async_remote_copy(
        src_ref=mrow.at[pl.ds(2, 2)], dst_ref=mh, send_sem=ms_sem, recv_sem=mr_sem,
        device_id={"band": to_band}, device_id_type=MESH,
    )

    @pl.when(has_send)
    def _():
        mask_copy.start()

    def halo(j):
        rows = rows_at(j)
        return pltpu.make_async_remote_copy(
            src_ref=hs.at[:, rows, :], dst_ref=hr.at[:, rows, :],
            send_sem=hs_sem, recv_sem=hr_sem.at[j],
            device_id={"band": to_band}, device_id_type=MESH,
        )

    mine = pl.ds(pl.multiple_of(half * HALF, 128), HALF)
    theirs = pl.ds(pl.multiple_of((1 - half) * HALF, 128), HALF)

    pieces = ((0, 32), (32, 32), (64, 32), (96, 16))

    def ring(block, step, n, k):
        part = C.at[block, pl.ds(*pieces[k]), mine]
        return pltpu.make_async_remote_copy(
            src_ref=part, dst_ref=part, send_sem=cs_sem, recv_sem=ring_sem.at[n, k],
            device_id={"band": (b + step + 32) % 16}, device_id_type=MESH,
        )

    xy = (
        y * 4 + (x + 1) % 4,
        y * 4 + (x + 3) % 4,
        ((y + 1) % 4) * 4 + x,
        ((y + 3) % 4) * 4 + x,
    )

    def turned(way):
        way = way % 4
        return jnp.where(way == 0, xy[0], jnp.where(way == 1, xy[2], jnp.where(way == 2, xy[1], xy[3])))

    def spread(block, at, k):
        for m, (lo, cnt) in enumerate((pieces[k],)):
            piece = C.at[block, pl.ds(lo, cnt), mine]
            pltpu.make_async_remote_copy(
                src_ref=piece, dst_ref=piece, send_sem=cs_sem, recv_sem=xy_sem.at[at],
                device_id={"comp": turned(k + at + core)}, device_id_type=MESH,
            ).start()

    def to_sib(block, n, rows=pl.ds(0, KP), cols=pl.ds(0, KALL)):
        part = C.at[block, rows, cols]
        return pltpu.make_async_remote_copy(
            src_ref=part, dst_ref=part, send_sem=cs_sem, recv_sem=sib_sem.at[n],
            device_id={"band": sib}, device_id_type=MESH,
        )

    events = [(1, s) for s in range(1, LAST[1] + 1)] + [(-1, s) for s in range(1, LAST[-1] + 1)]

    def block_of(side, s, base=None):
        base = b if base is None else base
        return (base + 2 * side * s * dirn + 32) % 16

    def distance(side, s):
        return (side * s * dirn + 8) % 8 - 1

    def ring_start(side, s, block):
        for k in range(4):
            ring(block, -2 * side * dirn, events.index((side, s)), k).start()

    def ring_event(side, s):
        n = events.index((side, s))
        block = block_of(side, s)
        for k in range(4):
            ring(block, 0, n, k).wait_recv()
            if s < LAST[side]:
                ring(block, -2 * side * dirn, events.index((side, s + 1)), k).start()
            spread(block, distance(side, s), k)
            to_sib(block, n, pl.ds(*pieces[k]), mine).start()

    def xy_event(side, s):
        n = events.index((side, s))
        block = block_of(side, s)
        whole = C.at[block, :, theirs]
        pltpu.make_async_copy(whole, whole, xy_sem.at[distance(side, s)]).wait()
        to_sib(block, n, cols=theirs).start()

    def sib_event(side, s):
        to_sib(block_of(side, s, sib), events.index((side, s))).wait_recv()

    def run(steps):
        for kind, side, s in steps:
            if kind == "start":
                ring_start(side, 1, b)
            else:
                {"ring": ring_event, "xy": xy_event, "sib": sib_event}[kind](side, s)

    run(AT_START)

    for j in range(NCH):
        count = CH if j < NCH - 1 else KD - CH * (NCH - 1)
        for i in range(ROWS):
            load(j, i).wait()
            v = wrap(raw[i, pl.ds(j * CH, count), :])
            if count < CH:
                v = jnp.concatenate([v, jnp.zeros((CH - count, LP), F32)], axis=0)
            f[3 + i, pl.ds(j * CH, CH), :] = v
            if i > 0:
                hs[i - 1, pl.ds(j * CH, CH), :] = v.astype(BF16)

        @pl.when(has_send)
        def _():
            halo(j).start()

    to_sib(b, 7).start()

    blowing = wind[...].astype(F32)
    cosw, sinw = wrap(cosine_of(blowing)), wrap(sine_of(blowing))
    for r in range(ROWS):
        for k, v in enumerate((seas, cosw, sinw)):
            aux[4 * k + row_of(r)] = jnp.broadcast_to(v[r : r + 1], (8, LP))

    shape = (KP, 128)
    comp = (row_iota(shape) + c * KD).astype(F32)
    direction = jnp.floor((comp + 0.5) * (1.0 / FREQS))
    picked = lane_iota(shape).astype(F32) == comp - FREQS * direction
    speeds = jnp.concatenate([gc[...], jnp.zeros((1, 128 - FREQS), F32)], axis=1)
    speed = jnp.sum(jnp.where(picked, speeds, 0.0), axis=1, keepdims=True)
    speed = jnp.where(row_iota(shape) < KD, speed, 0.0)
    cosd, sind = cosine_of(direction), sine_of(direction)
    coef[8] = cosd
    coef[9] = sind
    coef[7] = jnp.abs(speed * sind)
    along = jnp.abs(speed * cosd)
    plane = row_iota((8, 128))
    row = (b * ROWS + jnp.where(up, plane - 3, 6 - plane)).astype(F32)
    inverse = 1.0 / sine((90.0 - first_lat - 0.25 * (row + 0.5)) * (math.pi / 180.0))
    for p in range(7):
        coef[p] = along * inverse[p : p + 1]

    def wide(v, n):
        return jnp.concatenate([v] * n, axis=1)

    def pair_of(n):
        away, other = ORDER[0]
        for k in range(1, len(ORDER)):
            away = jnp.where(n == k, ORDER[k][0], away)
            other = jnp.where(n == k, ORDER[k][1], other)
        return ((y + jnp.where(core == 1, 4 - away, away)) % 4) * 2 + (x // 2 + other) % 2

    def advect(rows, shift):
        cols = [wide(coef[p, rows, :], LP // 128) for p in range(8)]
        for s in range(3):
            for p in range(6, s, -1):
                v = f[p, rows, :]
                moved = v - cols[p] * (v - pltpu.roll(v, shift, 1)) - cols[7] * (v - f[p - 1, rows, :])
                f[p, rows, :] = moved * (mask_h[p - 1] if p < 3 else aux[p - 3])

    eacc[...] = jnp.zeros_like(eacc)

    @pl.when(has_recv)
    def _():
        mask_copy.wait_recv()
        for p in range(2):
            mask_h[p] = jnp.broadcast_to(mh[p], (8, LP))

    @pl.when(jnp.logical_not(has_recv))
    def _():
        mask_h[...] = jnp.zeros_like(mask_h)

    @pl.loop(0, NCH)
    def _(j):
        rows = rows_at(j)

        @pl.when(has_recv)
        def _():
            halo(j).wait_recv()
            for p in range(3):
                f[p, rows, :] = hr[p, rows, :].astype(F32)

        @pl.when(jnp.logical_not(has_recv))
        def _():
            for p in range(3):
                f[p, rows, :] = jnp.zeros((CH, LP), F32)

        @pl.when(west)
        def _():
            for h in range(2):
                advect(pl.ds(pl.multiple_of(j * CH + 8 * h, 8), 8), 1)

        @pl.when(jnp.logical_not(west))
        def _():
            for h in range(2):
                advect(pl.ds(pl.multiple_of(j * CH + 8 * h, 8), 8), LP - 1)

        for i in range(ROWS):
            for q in range(4):
                lanes = pl.ds(q * QW, QW)
                v = f[3 + i, rows, lanes]
                eacc[i, :, lanes] = eacc[i, :, lanes] + v[:8] + v[8:]
                stage[4 * row_of(i) + q, rows, :] = (v * v).astype(BF16)

        @pl.when(j == NCH - 1)
        def _():
            at = row_iota((CH, QW))
            for i in range(ROWS):
                for q in range(4):
                    lanes = pl.ds(q * QW, QW)
                    total = jnp.sum(eacc[i, :, lanes], axis=0, keepdims=True)
                    hi = total.astype(BF16).astype(F32)
                    mid = (total - hi).astype(BF16).astype(F32)
                    lo = total - hi - mid
                    sq = stage[4 * row_of(i) + q, rows, :].astype(F32)
                    sq = jnp.where(at == 12, hi, jnp.where(at == 13, mid, jnp.where(at == 14, lo, sq)))
                    stage[4 * row_of(i) + q, rows, :] = sq.astype(BF16)

        place = pl.ds(pl.multiple_of(c * KP + j * CH, CH), CH)

        @pl.loop(0, len(ORDER))
        def _(n):
            for k in range(2):
                to = pair_of(n) * 2 + k

                @pl.when(to != c)
                def _():
                    pltpu.make_async_remote_copy(
                        src_ref=stage.at[to, rows, :], dst_ref=S.at[place, :],
                        send_sem=ss_sem, recv_sem=sr_sem,
                        device_id={"comp": to}, device_id_type=MESH,
                    ).start()

        for at, steps in DURING.items():
            @pl.when(j == at)
            def _(steps=steps):
                run(steps)

    S[pl.ds(pl.multiple_of(c * KP, CH), KP), :] = stage[c]
    run(BEFORE_S)
    to_sib(sib, 7).wait_recv()
    rest = S.at[pl.ds(0, (NB - 1) * KP), :]
    pltpu.make_async_copy(rest, rest, sr_sem).wait()
    run(AFTER_S)

    def back(to):
        return pltpu.make_async_remote_copy(
            src_ref=tst.at[to], dst_ref=trv.at[c], send_sem=ts_sem, recv_sem=tr_sem.at[c],
            device_id={"comp": to}, device_id_type=MESH,
        )

    def code(t):
        at = row_iota((KP, QW))
        mean = t[KD : KD + 1] * (1.0 / COMPS)
        t = jnp.maximum(t, -6.0)
        top = jnp.max(jnp.where(at < KD, jnp.abs(t), 0.0), axis=0, keepdims=True)
        power = jnp.ceil(jnp.log2(jnp.maximum(top, 1e-12)) + 0.01)
        scaled = t * (32000.0 * jnp.exp2(-power))
        hi = jnp.floor(mean * 16000.0)
        lo = (mean * 16000.0 - hi) * 32000.0
        scaled = jnp.where(at < KD, scaled, jnp.where(at == KD, power, jnp.where(at == KD + 1, hi, lo)))
        return jnp.round(scaled).astype(jnp.int32).astype(jnp.int16)

    def multiply(chip):
        lhs = C[pl.ds(chip * 2, 2)].reshape(2 * KP, KALL)
        t = jnp.dot(lhs, S[...], preferred_element_type=F32)
        for k in range(2):
            to = chip * 2 + k
            tst[to] = code(t[k * KP : (k + 1) * KP])

            @pl.when(to != c)
            def _():
                back(to).start()

    @pl.loop(0, len(ORDER))
    def _(n):
        multiply(pair_of(n))

    trv[c] = tst[c]

    def finish(i, q, width):
        r = row_of(i)
        o = 4 * r + q
        lanes = pl.ds(pl.multiple_of(q * QW, 128), QW)
        final_lanes = pl.ds(pl.multiple_of(q * QW, 128), width)

        @pl.when(o != c)
        def _():
            pltpu.make_async_copy(tst.at[o], trv.at[o], tr_sem.at[o]).wait()

        info = trv[o, pl.ds(KP - CH, CH), :].astype(jnp.int32).astype(F32)[8:]
        scale = jnp.broadcast_to(jnp.exp2(info)[4:5] * (step_time / 32000.0), (8, QW))
        energy = info[5:6] + info[6:7] * (1.0 / 32000.0)
        energy = jnp.broadcast_to(energy * (step_time * damping / 16000.0), (8, QW))
        mask = aux[i, :, lanes]
        cosw = aux[4 + i, :, lanes] * (step_time * wind_gain)
        sinw = aux[8 + i, :, lanes] * (step_time * wind_gain)
        for j in range(NCH):
            t = trv[o, pl.ds(j * CH, CH), :].astype(jnp.int32).astype(F32)
            for h in range(2):
                rows = pl.ds(j * CH + 8 * h, 8)
                v = f[3 + i, rows, lanes]
                facing = wide(coef[8, rows, :], 3) * cosw + wide(coef[9, rows, :], 3) * sinw
                new = v + (jnp.maximum(facing, 0.0) - energy) * v + t[8 * h : 8 * h + 8] * scale
                new = jnp.maximum(new, 0.0) * mask
                count = min(8, KD - (j * CH + 8 * h))
                raw[i, pl.ds(j * CH + 8 * h, count), final_lanes] = new[:count, :width]

    def result(i):
        return pltpu.make_async_copy(raw.at[i], out.at[:, row_of(i), :], out_sem.at[i])

    @pl.loop(0, ROWS)
    def _(i):
        @pl.loop(0, 3)
        def _(q):
            finish(i, q, QW)

        finish(i, 3, LON - 3 * QW)
        result(i).start()

    @pl.when(has_send)
    def _():
        mask_copy.wait_send()
        pltpu.make_async_copy(hs, hs, hs_sem).wait()

    sent = C.at[pl.ds(0, 15)]
    pltpu.make_async_copy(sent, sent, cs_sem).wait()
    pltpu.make_async_copy(rest, rest, ss_sem).wait()
    tsent = tst.at[pl.ds(0, 15)]
    pltpu.make_async_copy(tsent, tsent, ts_sem).wait()
    for i in range(ROWS):
        result(i).wait()


def hand_on(src, dst, held, sem, out_sem):
    first, second = [], []
    for k in range(4):
        part = pl.ds(k * (KD // 4), KD // 4)
        first.append(pltpu.make_async_copy(src.at[part], held.at[part], sem.at[k]))
        second.append(pltpu.make_async_copy(held.at[part], dst.at[part], out_sem.at[k]))
    for copy in first:
        copy.start()
    for k in range(4):
        first[k].wait()
        second[k].start()
    for copy in second:
        copy.wait()


def body(spectrum, group_courant, coupling, wind_dir, sea_mask, owner_cells, owner_counts):
    vmem = pl.BlockSpec(memory_space=pltpu.VMEM)
    hbm = pl.BlockSpec(memory_space=pl.ANY)
    dma = pltpu.SemaphoreType.DMA
    staged = pl.pallas_call(
        kernel,
        out_shape=jax.ShapeDtypeStruct((KD, ROWS, LON), F32),
        in_specs=[hbm, vmem, vmem, vmem, vmem],
        out_specs=hbm,
        scratch_shapes=[
            pltpu.VMEM((ROWS, KD, LON), F32),
            pltpu.VMEM((7, KP, LP), F32),
            pltpu.VMEM((3, KP, LP), BF16),
            pltpu.VMEM((3, KP, LP), BF16),
            pltpu.VMEM((10, KP, 128), F32),
            pltpu.VMEM((12, 8, LP), F32),
            pltpu.VMEM((ROWS, 1, LP), F32),
            pltpu.VMEM((2, 1, LP), F32),
            pltpu.VMEM((2, 8, LP), F32),
            pltpu.VMEM((NB, KP, QW), BF16),
            pltpu.VMEM((KALL, QW), BF16),
            pltpu.VMEM((NB, KP, KALL), BF16),
            pltpu.VMEM((NB, KP, QW), jnp.int16),
            pltpu.VMEM((NB, KP, QW), jnp.int16),
            pltpu.VMEM((ROWS, 8, LP), F32),
            dma((NCH, ROWS)), dma, dma((NCH,)), dma, dma, dma, dma, dma, dma((NB,)),
            dma, dma((7, 4)), dma((7,)), dma((8,)), dma((ROWS,)),
        ],
        compiler_params=pltpu.CompilerParams(
            collective_id=0, has_side_effects=True, vmem_limit_bytes=56 * 2**20
        ),
        cost_estimate=pl.CostEstimate(
            flops=2 * KALL * KALL * QW, bytes_accessed=12 * 2**20, transcendentals=0
        ),
    )(spectrum, group_courant.reshape(1, FREQS), coupling, wind_dir, sea_mask)
    return pl.pallas_call(
        hand_on,
        out_shape=jax.ShapeDtypeStruct((KD, ROWS, LON), F32),
        in_specs=[hbm],
        out_specs=hbm,
        scratch_shapes=[pltpu.VMEM((KD, ROWS, LON), F32), dma((4,)), dma((4,))],
    )(staged)


def solution(mesh):
    return jax.shard_map(
        body,
        mesh=mesh,
        in_specs=(
            P("comp", "band", None),
            P(),
            P("band", None),
            P("band", None),
            P("band", None),
            P(("band", "comp"), None),
            P(("band", "comp")),
        ),
        out_specs=P("comp", "band", None),
        check_vma=False,
    )
```
